32 devices in a mesh: parts: 2 (over x), store: 8 (over z, y), tensor: 2 (over core).
Axes of the slice: x: 2, y: 2, z: 4, core: 2. Of those that a mesh axis runs over, the one named last changes fastest.
Arguments:
- hidden: bfloat16 [512, 28672], P(('parts', 'store'), 'tensor'), parts along dimension 0, may hold values from -6 to 6
- down_weight: bfloat16 [28672, 8192], P('tensor', 'store'), may hold values from -0.03125 to 0.03125
- shrink_weight: bfloat16 [32, 28672, 64], P(('parts', 'store'), 'tensor'), parts along dimension 0, may hold values from -0.03125 to 0.03125
- expand_weight: bfloat16 [32, 64, 8192], P(('parts', 'store')), parts along dimension 0, may hold values from -0.75 to 0.75
- row_adapter: int32 [512], P('parts'), parts along dimension 0, may hold values from 0 to 15
- adapter_slot: int32 [32], P('parts'), parts along dimension 0, may hold values from 0 to 15, each once
Outputs:
- mixed: bfloat16 [512, 8192], P('parts', ('store', 'tensor')), parts along dimension 0
The draws below stay inside these ranges and needn't reach their ends.
There are 2 independent parts, one for each index of `parts`. The reference program is written for one: setup_inputs(seed, part) draws one part's arguments, and reference() takes and returns one part's arrays. A program takes and returns all parts, laid end to end along the dimension named above; an argument that names none is the same for every part. Nothing has to cross between parts.
Inputs may be any that keep to these rules, and one draw needn't show every extreme that they name: `row_adapter`: every row names one of the 16 adapter ids. `adapter_slot`: each storage slot holds exactly one adapter id.
All inputs are finite; a program needn't handle non-finite values.
Results may differ from the reference program's by a relative error of at most 0.004.
Values may be sent and summed in bfloat16 or wider, within the bound.
No kernel may reach another device: no remote copies, remote signals or barrier semaphores. Data moves between devices by JAX's collectives and lax.ppermute only.
A program may use at most 128 MiB of HBM per device.

```python
import math
import jax
import jax.numpy as jnp
import numpy as np

D = 8192
FF = 28672
RANK = 64
ROWS = 256
ADAPTERS = 16


def plant(drawn, key, smallest, largest):
    index_at = [jax.random.randint(jax.random.fold_in(key, axis), (), 0, length) for axis, length in enumerate(drawn.shape)]
    widest = drawn.shape.index(max(drawn.shape))
    beside = index_at[:widest] + [(index_at[widest] + 1) % drawn.shape[widest]] + index_at[widest + 1:]
    return drawn.at[tuple(index_at)].set(smallest).at[tuple(beside)].set(largest)


def shard_levels(rng, extent, pieces, low, largest):
    factor_of, own = 1.0, jax.random.fold_in(rng, 6)
    for axis_at, blocks in pieces:
        steps = jnp.exp(jax.random.uniform(jax.random.fold_in(own, axis_at), (blocks,), jnp.float32, low / len(pieces), largest / len(pieces)))
        factor_of = factor_of * jnp.repeat(steps, extent[axis_at] // blocks).reshape([-1 if axis == axis_at else 1 for axis in range(len(extent))])
    return factor_of


def rank_table(number_of, slope):
    weights = [(1 << 20) // math.isqrt(rank ** slope) + 1 for rank in range(1, number_of + 1)]
    deviation = 1 + sum(weights) // (1 << 30)
    return np.cumsum(np.array([max(1, weight // deviation) for weight in weights]))


def ranked_ids(own_key, extent, count, skew):
    table = rank_table(count, skew)
    lot = jax.random.randint(jax.random.fold_in(own_key, 1), extent, 0, int(table[count - 1]))
    standing = jnp.searchsorted(jnp.asarray(table, jnp.int32), lot, side="right")
    return jax.random.permutation(jax.random.fold_in(own_key, 2), count)[standing].astype(jnp.int32)


def normal_values(stream_key, dims, scale, limit, pieces=(), kind=jnp.bfloat16):
    loudness = shard_levels(stream_key, dims, pieces, -0.22, 0.18) if pieces else 1.0
    entries = jax.random.normal(stream_key, dims, jnp.float32) * scale * loudness
    return jnp.minimum(jnp.maximum(entries, -limit), limit).astype(kind)


def setup_inputs(seed: int = 0, part: int = 0) -> dict:
    streams_of = jax.random.split(jax.random.key(seed), 7)
    part_splits = jax.random.split(jax.random.fold_in(streams_of[6], part), 7)
    hidden = normal_values(part_splits[0], (ROWS, FF), 1.0, 6.0, ((0, 8), (1, 2)))
    down_weight = normal_values(streams_of[1], (FF, D), FF ** -0.5, 0.03125, ((0, 2), (1, 8)))
    shrink_weight = normal_values(part_splits[2], (ADAPTERS, FF, RANK), FF ** -0.5, 0.03125, ((0, 8), (1, 2)))
    expand_weight = normal_values(part_splits[3], (ADAPTERS, RANK, D), RANK ** -0.5, 0.75, ((0, 8),))
    row_adapter = plant(ranked_ids(part_splits[4], (ROWS,), ADAPTERS, 2), jax.random.fold_in(part_splits[4], 3), 0, ADAPTERS - 1).astype(jnp.int32)
    adapter_slot = jax.random.permutation(part_splits[5], ADAPTERS).astype(jnp.int32)
    return {"hidden": hidden, "down_weight": down_weight, "shrink_weight": shrink_weight, "expand_weight": expand_weight, "row_adapter": row_adapter, "adapter_slot": adapter_slot}


def reference(hidden, down_weight, shrink_weight, expand_weight, row_adapter, adapter_slot):
    base = jnp.dot(hidden, down_weight, preferred_element_type=jnp.float32)
    row_slot = adapter_slot[row_adapter].astype(jnp.int32)
    stacked = jnp.transpose(shrink_weight, (1, 0, 2)).reshape(FF, ADAPTERS * RANK)
    every = jnp.dot(hidden, stacked, preferred_element_type=jnp.float32).reshape(ROWS, ADAPTERS, RANK)
    picks = row_slot[:, None] == jnp.arange(ADAPTERS, dtype=jnp.int32)[None, :]
    shrunk = jnp.sum(jnp.where(picks[:, :, None], every, jnp.zeros((), jnp.float32)), axis=1).astype(jnp.bfloat16)
    spread = jnp.where(picks[:, :, None], shrunk[:, None, :], jnp.zeros((), jnp.bfloat16)).reshape(ROWS, ADAPTERS * RANK)
    extra = jnp.dot(spread, expand_weight.reshape(ADAPTERS * RANK, D), preferred_element_type=jnp.float32)
    return (base + extra).astype(jnp.bfloat16)
```

```python
import functools

import jax
import jax.numpy as jnp
from jax import lax
from jax.experimental import pallas as pl
from jax.experimental.pallas import tpu as pltpu
from jax.sharding import PartitionSpec as P

F32, BF16 = jnp.float32, jnp.bfloat16
CHUNKS = 4
VMEM = 48 * 2**20


def ring_order(n):
    return list(range(0, n, 2)) + list(range(1, n, 2))[::-1]


def split_kernel(place, src, dst):
    dst[...] = src[...][None]


def expand_blocks(expand, n, parts_of_columns, tensor_place):
    owned, rank, width = expand.shape
    rows = owned * rank
    share = width // (n * parts_of_columns)
    return pl.pallas_call(
        split_kernel,
        grid_spec=pltpu.PrefetchScalarGridSpec(
            num_scalar_prefetch=1,
            grid=(n,),
            in_specs=[pl.BlockSpec((rows, share), lambda s, t: (0, s * parts_of_columns + t[0]))],
            out_specs=pl.BlockSpec((1, rows, share), lambda s, t: (s, 0, 0)),
        ),
        out_shape=jax.ShapeDtypeStruct((n, rows, share), BF16),
        compiler_params=pltpu.CompilerParams(vmem_limit_bytes=VMEM),
        cost_estimate=pl.CostEstimate(flops=0, bytes_accessed=4 * n * rows * share, transcendentals=0),
        name="expand_blocks",
    )(tensor_place.reshape(1), expand.reshape(rows, width))


def matmul_kernel(n, steps, has_narrow, sides, has_acc, owned, places, *refs):
    refs = list(refs)
    pieces = [refs.pop(0) for _ in range(n)]
    weights = [refs.pop(0) for _ in range(sides)]
    shrink = refs.pop(0) if has_narrow else None
    count = sides + (1 if has_narrow else 0)
    before = [refs.pop(0) for _ in range(count)] if has_acc else None
    after = [refs.pop(0) for _ in range(count)]
    lhs = refs.pop(0)
    step = pl.program_id(0)
    rows = pieces[0].shape[0]

    @pl.when(step == 0)
    def _():
        for i in range(count):
            after[i][...] = before[i][...] if has_acc else jnp.zeros_like(after[i])

    for i in range(n):
        at = pl.multiple_of(places[i] * rows, rows)
        lhs[pl.ds(at, rows), :] = pieces[i][...]
    if has_narrow:
        after[-1][...] += lax.dot_general(
            shrink[...], lhs[...], (((1,), (1,)), ((), ())), preferred_element_type=F32
        )
    for i in range(sides):
        after[i][...] += jnp.dot(lhs[...], weights[i][...], preferred_element_type=F32)


def chunk_matmul(scalars, pieces, down, shrink, acc, chunk, width, tile, sides, narrow, label):
    n = len(pieces)
    rows = pieces[0].shape[0] * n
    share = down.shape[1] // 2
    steps = width // tile
    first = chunk * steps
    narrow_rows = shrink.shape[0]
    in_specs = [pl.BlockSpec((rows // n, tile), lambda k, s: (0, k)) for _ in pieces]
    args = list(pieces)
    for side in sides:
        in_specs.append(pl.BlockSpec((tile, share), functools.partial(lambda side, k, s: (first + k, s[n + side]), side)))
        args.append(down)
    if narrow:
        in_specs.append(pl.BlockSpec((narrow_rows, tile), lambda k, s: (0, first + k)))
        args.append(shrink)
    shapes = [(rows, share)] * len(sides) + ([(narrow_rows, rows)] if narrow else [])
    whole = [pl.BlockSpec(shape, lambda k, s: (0, 0)) for shape in shapes]
    aliases = {}
    if acc is not None:
        aliases = {1 + len(args) + i: i for i in range(len(shapes))}
        in_specs += whole
        args += list(acc)
    columns = share * len(sides) + (narrow_rows if narrow else 0)
    return pl.pallas_call(
        functools.partial(matmul_kernel, n, steps, narrow, len(sides), acc is not None, 0),
        grid_spec=pltpu.PrefetchScalarGridSpec(
            num_scalar_prefetch=1,
            grid=(steps,),
            in_specs=in_specs,
            out_specs=whole,
            scratch_shapes=[pltpu.VMEM((rows, tile), BF16)],
        ),
        out_shape=[jax.ShapeDtypeStruct(shape, F32) for shape in shapes],
        input_output_aliases=aliases,
        compiler_params=pltpu.CompilerParams(vmem_limit_bytes=VMEM),
        cost_estimate=pl.CostEstimate(
            flops=2 * rows * width * columns,
            bytes_accessed=2 * width * (columns + rows) + 8 * rows * columns,
            transcendentals=0,
        ),
        name=label,
    )(scalars, *args)


def final_kernel(n, rank, owned, owners, *refs):
    pieces, (slot, factors, kept, other, out, spread) = refs[:n], refs[n:]
    wide = owned * rank
    lane = lax.broadcasted_iota(jnp.int32, (out.shape[0], wide), 1) // rank
    for i in range(n):
        owner = owners[i]
        own = pieces[i][...].astype(F32).T
        pair = jnp.concatenate([own] * owned, axis=1)
        block = jnp.where(slot[...] == owner * owned + lane, pair, 0.0).astype(BF16)
        spread[:, i * wide:(i + 1) * wide] = block
    total = kept[...] + other[...]
    for i in range(n):
        total += jnp.dot(spread[:, i * wide:(i + 1) * wide], factors[owners[i]], preferred_element_type=F32)
    out[...] = total.astype(BF16)


def final(owners, pieces, slot_column, factors, kept, other, owned):
    n = len(pieces)
    rank = pieces[0].shape[0]
    rows, share = kept.shape
    return pl.pallas_call(
        functools.partial(final_kernel, n, rank, owned),
        grid_spec=pltpu.PrefetchScalarGridSpec(
            num_scalar_prefetch=1,
            grid=(1,),
            in_specs=[pl.BlockSpec(p.shape, lambda k, s: (0, 0)) for p in pieces]
            + [
                pl.BlockSpec((rows, 1), lambda k, s: (0, 0)),
                pl.BlockSpec(factors.shape, lambda k, s: (0, 0, 0)),
                pl.BlockSpec((rows, share), lambda k, s: (0, 0)),
                pl.BlockSpec((rows, share), lambda k, s: (0, 0)),
            ],
            out_specs=pl.BlockSpec((rows, share), lambda k, s: (0, 0)),
            scratch_shapes=[pltpu.VMEM((rows, n * owned * rank), BF16)],
        ),
        out_shape=jax.ShapeDtypeStruct((rows, share), BF16),
        compiler_params=pltpu.CompilerParams(vmem_limit_bytes=VMEM),
        cost_estimate=pl.CostEstimate(
            flops=2 * rows * share * n * owned * rank,
            bytes_accessed=2 * n * owned * rank * share + 10 * rows * share,
            transcendentals=0,
        ),
        name="expand_and_add",
    )(owners, *pieces, slot_column, factors, kept, other)


def make_shards(n, cores):
    order = ring_order(n)
    place_of = {store: place for place, store in enumerate(order)}
    clockwise = [(order[i], order[(i + 1) % n]) for i in range(n)]
    counter = [(order[i], order[i - 1]) for i in range(n)]
    long, short = n // 2, (n - 1) // 2
    swap = [(t, (t + 1) % cores) for t in range(cores)]

    def shards(hidden, down, shrink, expand, row_adapter, adapter_slot):
        owned, units, rank = shrink.shape
        width = units // CHUNKS
        tile = width // 7
        store, tensor = lax.axis_index("store"), lax.axis_index("tensor")
        place = jnp.asarray([place_of[s] for s in range(n)], jnp.int32)[store]
        at = jnp.asarray(order, jnp.int32)
        shrink_rows = jnp.transpose(shrink, (0, 2, 1)).reshape(owned * rank, units)

        blocks = expand_blocks(expand, n, cores, tensor)
        slots = jnp.arange(adapter_slot.shape[0], dtype=jnp.int32)
        row_slot = jnp.sum(jnp.where(row_adapter[None, :] == slots[:, None], adapter_slot[:, None], 0), axis=0)

        acc = None
        for chunk in range(CHUNKS):
            own = hidden[:, chunk * width:(chunk + 1) * width]
            steps = (long, short) if chunk % 2 == 0 else (short, long)
            pieces, shifts = [own], [0]
            for length, pairs, sign in zip(steps, (clockwise, counter), (-1, 1)):
                moving = own
                for step in range(1, length + 1):
                    moving = lax.ppermute(moving, "store", pairs)
                    pieces.append(moving)
                    shifts.append(sign * step)
            places = at[(place + jnp.asarray(shifts, jnp.int32)) % n]
            scalars = jnp.concatenate([places, jnp.stack([tensor, 1 - tensor])]).astype(jnp.int32)
            if chunk < CHUNKS - 1:
                acc = chunk_matmul(scalars, pieces, down, shrink_rows, acc, chunk, width, tile, (0, 1), True, f"chunk_{chunk}")
            else:
                send, narrow = chunk_matmul(
                    scalars, pieces, down, shrink_rows, acc and acc[1:], chunk, width, tile, (1,), True, "last_sent"
                )
                kept, = chunk_matmul(
                    scalars, pieces, down, shrink_rows, acc and acc[:1], chunk, width, tile, (0,), False, "last_kept"
                )
        mine = [
            jnp.where((row_slot == store * owned + i)[None, :], narrow[i * rank:(i + 1) * rank], 0.0)
            for i in range(owned)
        ]
        mine = sum(mine[1:], mine[0])
        shrunk = (mine + lax.ppermute(mine, "tensor", swap)).astype(BF16)
        other = lax.ppermute(send, "tensor", swap)
        everyone, owners = [shrunk], [store]
        for shift in range(1, n):
            everyone.append(lax.ppermute(shrunk, "store", [(s, (s + shift) % n) for s in range(n)]))
            owners.append((store - shift) % n)
        factors = lax.all_to_all(blocks, "store", 0, 0)
        return final(jnp.stack(owners).astype(jnp.int32), everyone, row_slot[:, None], factors, kept, other, owned)

    return shards


def solution(mesh):
    in_specs = (
        P(("parts", "store"), "tensor"),
        P("tensor", "store"),
        P(("parts", "store"), "tensor", None),
        P(("parts", "store"), None, None),
        P("parts"),
        P("parts"),
    )
    out_specs = P("parts", ("store", "tensor"))
    shards = make_shards(mesh.shape["store"], mesh.shape["tensor"])
    return jax.shard_map(shards, mesh=mesh, in_specs=in_specs, out_specs=out_specs, check_vma=False)
```

```python
import functools

import jax
import jax.numpy as jnp
import numpy as np
from jax import lax
from jax.experimental import pallas as pl
from jax.experimental.pallas import tpu as pltpu
from jax.sharding import PartitionSpec as P

F32, BF16 = jnp.float32, jnp.bfloat16
TILE = 512
MIB = 2**20


def params(mib):
    return pltpu.CompilerParams(vmem_limit_bytes=mib * MIB)


def ring_order(n):
    return list(range(0, n, 2)) + list(range(1, n, 2))[::-1]


def take_kernel(start, width, src, *refs):
    *_, dst, sem = refs
    copy = pltpu.make_async_copy(src.at[:, pl.ds(start, width)], dst, sem)
    copy.start()
    copy.wait()


def take(hidden, start, width, after):
    rows = hidden.shape[0]
    return pl.pallas_call(
        functools.partial(take_kernel, start, width),
        in_specs=[pl.BlockSpec(memory_space=pl.ANY)] * (1 + len(after)),
        out_specs=pl.BlockSpec(memory_space=pl.ANY),
        scratch_shapes=[pltpu.SemaphoreType.DMA],
        out_shape=jax.ShapeDtypeStruct((rows, width), BF16),
        compiler_params=params(1),
        cost_estimate=pl.CostEstimate(flops=0, bytes_accessed=4 * rows * width, transcendentals=0),
        name=f"take_{start}",
    )(hidden, *after)


def split_kernel(scalars, src, after, dst):
    dst[...] = src[...][None]


def expand_blocks(scalars, half, expand, n, cores, after):
    owned, rank, width = expand.shape
    rows = owned * rank
    share = width // (n * cores)
    return pl.pallas_call(
        split_kernel,
        grid_spec=pltpu.PrefetchScalarGridSpec(
            num_scalar_prefetch=1,
            grid=(n,),
            in_specs=[
                pl.BlockSpec((rows, share), lambda s, t: (0, s * cores + t[half])),
                pl.BlockSpec(memory_space=pl.ANY),
            ],
            out_specs=pl.BlockSpec((1, rows, share), lambda s, t: (s, 0, 0)),
        ),
        out_shape=jax.ShapeDtypeStruct((n, rows, share), BF16),
        compiler_params=params(8),
        cost_estimate=pl.CostEstimate(flops=0, bytes_accessed=4 * n * rows * share, transcendentals=0),
        name="expand_blocks",
    )(scalars, expand.reshape(rows, width), after)


def matmul_kernel(n, base, sides, narrow, has_acc, scalars, *refs):
    refs = list(refs)
    pieces = [refs.pop(0) for _ in range(n)]
    weights = [refs.pop(0) for _ in range(sides)]
    shrink = refs.pop(0) if narrow else None
    count = sides + narrow
    before = [refs.pop(0) for _ in range(count)] if has_acc else None
    after = [refs.pop(0) for _ in range(count)]
    lhs, sems = refs
    step = pl.program_id(0)
    rows = pieces[0].shape[0]
    tile = lhs.shape[2]

    @pl.when(step == 0)
    def _():
        copies = []
        for i in range(n):
            at = pl.multiple_of(scalars[base + i] * rows, rows)
            for j in range(lhs.shape[0]):
                copies.append(
                    pltpu.make_async_copy(
                        pieces[i].at[:, pl.ds(j * tile, tile)], lhs.at[j, pl.ds(at, rows), :], sems.at[i, j]
                    )
                )
        for copy in copies:
            copy.start()
        for i in range(count):
            after[i][...] = before[i][...] if has_acc else jnp.zeros_like(after[i])
        for copy in copies:
            copy.wait()

    left = lhs[step]
    if narrow:
        after[-1][...] += lax.dot_general(
            shrink[...], left, (((1,), (1,)), ((), ())), preferred_element_type=F32
        )
    for i in range(sides):
        after[i][...] += jnp.dot(left, weights[i][...], preferred_element_type=F32)


def chunk_matmul(scalars, base, half, pieces, down, shrink, acc, start, sides, narrow, label):
    n = len(pieces)
    rows, width = pieces[0].shape[0] * n, pieces[0].shape[1]
    share = down.shape[1] // 2
    steps = width // TILE
    first = start // TILE
    ranks = shrink.shape[0]
    in_specs = [pl.BlockSpec(memory_space=pl.ANY) for _ in pieces]
    args = list(pieces)
    for side in sides:
        in_specs.append(pl.BlockSpec((TILE, share), functools.partial(lambda side, k, s: (first + k, s[half + side]), side)))
        args.append(down)
    if narrow:
        in_specs.append(pl.BlockSpec((ranks, TILE), lambda k, s: (0, first + k)))
        args.append(shrink)
    shapes = [(rows, share)] * len(sides) + [(ranks, rows)] * narrow
    whole = [pl.BlockSpec(shape, lambda k, s: (0, 0)) for shape in shapes]
    aliases = {}
    if acc is not None:
        aliases = {1 + len(args) + i: i for i in range(len(shapes))}
        in_specs += whole
        args += list(acc)
    columns = share * len(sides) + ranks * narrow
    return pl.pallas_call(
        functools.partial(matmul_kernel, n, base, len(sides), narrow, acc is not None),
        grid_spec=pltpu.PrefetchScalarGridSpec(
            num_scalar_prefetch=1,
            grid=(steps,),
            in_specs=in_specs,
            out_specs=whole,
            scratch_shapes=[pltpu.VMEM((steps, rows, TILE), BF16), pltpu.SemaphoreType.DMA((n, steps))],
        ),
        out_shape=[jax.ShapeDtypeStruct(shape, F32) for shape in shapes],
        input_output_aliases=aliases,
        compiler_params=params(24),
        cost_estimate=pl.CostEstimate(
            flops=4 * rows * width * columns,
            bytes_accessed=2 * width * (columns + rows) + 8 * rows * columns,
            transcendentals=0,
        ),
        name=label,
    )(scalars, *args)


def final_kernel(n, owned, shrunk, slot, factors, kept, other, out, spread):
    rank = shrunk.shape[0]
    wide = owned * rank
    rows = out.shape[0]
    lane = lax.broadcasted_iota(jnp.int32, (rows, wide), 1) // rank
    own = shrunk[...].astype(F32).T
    pair = jnp.concatenate([own] * owned, axis=1)
    place = slot[...] - lane
    for i in range(n):
        spread[:, i * wide:(i + 1) * wide] = jnp.where(place == i * owned, pair, 0.0).astype(BF16)
    extra = jnp.dot(spread[...], factors[...], preferred_element_type=F32)
    out[...] = (kept[...] + other[...] + extra).astype(BF16)


def final(shrunk, slot_column, factors, kept, other, owned):
    n, wide, share = factors.shape
    rows = kept.shape[0]
    return pl.pallas_call(
        functools.partial(final_kernel, n, owned),
        in_specs=[pl.BlockSpec(memory_space=pltpu.VMEM)] * 5,
        out_specs=pl.BlockSpec(memory_space=pltpu.VMEM),
        scratch_shapes=[pltpu.VMEM((rows, n * wide), BF16)],
        out_shape=jax.ShapeDtypeStruct((rows, share), BF16),
        compiler_params=params(24),
        cost_estimate=pl.CostEstimate(
            flops=2 * rows * share * n * wide,
            bytes_accessed=2 * n * wide * share + 10 * rows * share,
            transcendentals=0,
        ),
        name="expand_and_add",
    )(shrunk, slot_column, factors.reshape(n * wide, share), kept, other)


def make_shards(n, cores):
    order = ring_order(n)
    place_of = {store: place for place, store in enumerate(order)}
    clockwise = [(order[i], order[(i + 1) % n]) for i in range(n)]
    counter = [(order[i], order[i - 1]) for i in range(n)]
    long, short = n // 2, (n - 1) // 2
    swap = [(t, (t + 1) % cores) for t in range(cores)]
    hops = [[0] + [-i for i in range(1, a + 1)] + list(range(1, b + 1)) for a, b in ((long, short), (short, long))]
    table = np.array(
        [
            [order[(place_of[s] + hop) % n] for way in hops for hop in way] + [t, 1 - t]
            for s in range(n)
            for t in range(cores)
        ],
        np.int32,
    )
    half = 2 * n

    def shards(hidden, down, shrink, expand, row_adapter, adapter_slot):
        owned, units, rank = shrink.shape
        store, tensor = lax.axis_index("store"), lax.axis_index("tensor")
        scalars = lax.dynamic_slice_in_dim(jnp.asarray(table), store * cores + tensor, 1, 0)[0]
        shrink_rows = jnp.transpose(shrink, (0, 2, 1)).reshape(owned * rank, units)

        slots = jnp.arange(adapter_slot.shape[0], dtype=jnp.int32)
        row_slot = jnp.sum(jnp.where(row_adapter[None, :] == slots[:, None], adapter_slot[:, None], 0), axis=0)

        tiles = units // TILE
        small = tiles // 7
        widths = [(tiles - small) // 3 * TILE] * 3 + [small * TILE]
        widths[0] += units - sum(widths)

        acc, ends = None, []
        start = 0
        for chunk, width in enumerate(widths):
            own = hidden[:, :width] if chunk == 0 else take(hidden, start, width, after)
            way = chunk % 2
            pieces = [own]
            for length, pairs in zip(((long, short), (short, long))[way], (clockwise, counter)):
                moving = own
                for step in range(length):
                    moving = lax.ppermute(moving, "store", pairs)
                    pieces.append(moving)
            turn = (long, short)[way]
            after = [pieces[2], pieces[turn + 2], *ends]
            ends = [pieces[turn], pieces[-1]]
            if chunk == 1:
                after.append(blocks)
            if chunk == 2:
                after.append(factors)
            if chunk == 0:
                blocks = expand_blocks(scalars, half, expand, n, cores, pieces[1])
                factors = lax.all_to_all(blocks, "store", 0, 0)
            call = functools.partial(chunk_matmul, scalars, way * n, half, pieces, down, shrink_rows)
            if chunk < len(widths) - 1:
                acc = call(acc, start, (0, 1), True, f"chunk_{chunk}")
            else:
                narrow, = call(acc[2:], start, (), True, "last_narrow")
                send, = call(acc[1:2], start, (1,), False, "last_sent")
                kept, = call(acc[:1], start, (0,), False, "last_kept")
            start += width
        mine = [
            jnp.where((row_slot == store * owned + i)[None, :], narrow[i * rank:(i + 1) * rank], 0.0)
            for i in range(owned)
        ]
        mine = sum(mine[1:], mine[0])
        shrunk = (mine + lax.ppermute(mine, "tensor", swap)).astype(BF16)
        other = lax.ppermute(send, "tensor", swap)
        bit = 1
        while bit < n:
            shrunk = shrunk + lax.ppermute(shrunk, "store", [(s, s ^ bit) for s in range(n)])
            bit *= 2
        return final(shrunk, row_slot[:, None], factors, kept, other, owned)

    return shards


def solution(mesh):
    in_specs = (
        P(("parts", "store"), "tensor"),
        P("tensor", "store"),
        P(("parts", "store"), "tensor", None),
        P(("parts", "store"), None, None),
        P("parts"),
        P("parts"),
    )
    out_specs = P("parts", ("store", "tensor"))
    shards = make_shards(mesh.shape["store"], mesh.shape["tensor"])
    return jax.shard_map(shards, mesh=mesh, in_specs=in_specs, out_specs=out_specs, check_vma=False)
```

```python
import functools

import jax
import jax.numpy as jnp
import numpy as np
from jax import lax
from jax.experimental import pallas as pl
from jax.experimental.pallas import tpu as pltpu
from jax.sharding import PartitionSpec as P

F32, BF16 = jnp.float32, jnp.bfloat16
TILE = 1024
MIB = 2**20


def params(mib):
    return pltpu.CompilerParams(vmem_limit_bytes=mib * MIB)


def ring_order(n):
    return list(range(0, n, 2)) + list(range(1, n, 2))[::-1]


def take_kernel(start, width, src, *refs):
    *_, dst, sem = refs
    copy = pltpu.make_async_copy(src.at[:, pl.ds(start, width)], dst, sem)
    copy.start()
    copy.wait()


def take(hidden, start, width, after):
    rows = hidden.shape[0]
    return pl.pallas_call(
        functools.partial(take_kernel, start, width),
        in_specs=[pl.BlockSpec(memory_space=pl.ANY)] * (1 + len(after)),
        out_specs=pl.BlockSpec(memory_space=pl.ANY),
        scratch_shapes=[pltpu.SemaphoreType.DMA],
        out_shape=jax.ShapeDtypeStruct((rows, width), BF16),
        compiler_params=params(40),
        cost_estimate=pl.CostEstimate(flops=0, bytes_accessed=4 * rows * width, transcendentals=0),
        name=f"take_{start}",
    )(hidden, *after)


def split_kernel(scalars, src, dst):
    dst[...] = src[...][None]


def expand_blocks(scalars, half, expand, n, cores):
    owned, rank, width = expand.shape
    rows = owned * rank
    share = width // (n * cores)
    return pl.pallas_call(
        split_kernel,
        grid_spec=pltpu.PrefetchScalarGridSpec(
            num_scalar_prefetch=1,
            grid=(n,),
            in_specs=[pl.BlockSpec((rows, share), lambda s, t: (0, s * cores + t[half]))],
            out_specs=pl.BlockSpec((1, rows, share), lambda s, t: (s, 0, 0)),
        ),
        out_shape=jax.ShapeDtypeStruct((n, rows, share), BF16),
        compiler_params=params(40),
        cost_estimate=pl.CostEstimate(flops=0, bytes_accessed=4 * n * rows * share, transcendentals=0),
        name="expand_blocks",
    )(scalars, expand.reshape(rows, width))


def matmul_kernel(n, base, sides, narrow, has_acc, waits, scalars, *refs):
    refs = list(refs)[waits:]
    pieces = [refs.pop(0) for _ in range(n)]
    weights = [refs.pop(0) for _ in range(sides)]
    shrink = refs.pop(0) if narrow else None
    count = sides + narrow
    before = [refs.pop(0) for _ in range(count)] if has_acc else None
    after = [refs.pop(0) for _ in range(count)]
    lhs, sems = refs
    step = pl.program_id(0)
    rows = pieces[0].shape[0]
    tile = lhs.shape[2]

    @pl.when(step == 0)
    def _():
        copies = []
        for i in range(n):
            at = pl.multiple_of(scalars[base + i] * rows, rows)
            for j in range(lhs.shape[0]):
                copies.append(
                    pltpu.make_async_copy(
                        pieces[i].at[:, pl.ds(j * tile, tile)], lhs.at[j, pl.ds(at, rows), :], sems.at[i, j]
                    )
                )
        for copy in copies:
            copy.start()
        for i in range(count):
            after[i][...] = before[i][...] if has_acc else jnp.zeros_like(after[i])
        for copy in copies:
            copy.wait()

    left = lhs[step]
    if narrow:
        after[-1][...] += lax.dot_general(
            shrink[...], left, (((1,), (1,)), ((), ())), preferred_element_type=F32
        )
    for i in range(sides):
        after[i][...] += jnp.dot(left, weights[i][...], preferred_element_type=F32)


def chunk_matmul(scalars, base, half, pieces, down, shrink, acc, start, sides, narrow, label, after=()):
    n = len(pieces)
    rows, width = pieces[0].shape[0] * n, pieces[0].shape[1]
    share = down.shape[1] // 2
    steps = width // TILE
    first = start // TILE
    ranks = shrink.shape[0]
    in_specs = [pl.BlockSpec(memory_space=pl.ANY) for _ in (*after, *pieces)]
    args = [*after, *pieces]
    for side in sides:
        in_specs.append(pl.BlockSpec((TILE, share), functools.partial(lambda side, k, s: (first + k, s[half + side]), side)))
        args.append(down)
    if narrow:
        in_specs.append(pl.BlockSpec((ranks, TILE), lambda k, s: (0, first + k)))
        args.append(shrink)
    shapes = [(rows, share)] * len(sides) + [(ranks, rows)] * narrow
    whole = [pl.BlockSpec(shape, lambda k, s: (0, 0)) for shape in shapes]
    aliases = {}
    if acc is not None:
        aliases = {1 + len(args) + i: i for i in range(len(shapes))}
        in_specs += whole
        args += list(acc)
    columns = share * len(sides) + ranks * narrow
    return pl.pallas_call(
        functools.partial(matmul_kernel, n, base, len(sides), narrow, acc is not None, len(after)),
        grid_spec=pltpu.PrefetchScalarGridSpec(
            num_scalar_prefetch=1,
            grid=(steps,),
            in_specs=in_specs,
            out_specs=whole,
            scratch_shapes=[pltpu.VMEM((steps, rows, TILE), BF16), pltpu.SemaphoreType.DMA((n, steps))],
        ),
        out_shape=[jax.ShapeDtypeStruct(shape, F32) for shape in shapes],
        input_output_aliases=aliases,
        compiler_params=params(40),
        cost_estimate=pl.CostEstimate(
            flops=4 * rows * width * columns,
            bytes_accessed=2 * width * (columns + rows) + 8 * rows * columns,
            transcendentals=0,
        ),
        name=label,
    )(scalars, *args)


def final_kernel(n, owned, shrunk, slot, factors, kept, other, out, spread):
    rank = shrunk.shape[0]
    wide = owned * rank
    rows = out.shape[0]
    lane = lax.broadcasted_iota(jnp.int32, (rows, wide), 1) // rank
    own = shrunk[...].astype(F32).T
    pair = jnp.concatenate([own] * owned, axis=1)
    place = slot[...] - lane
    for i in range(n):
        spread[:, i * wide:(i + 1) * wide] = jnp.where(place == i * owned, pair, 0.0).astype(BF16)
    extra = jnp.dot(spread[...], factors[...], preferred_element_type=F32)
    out[...] = (kept[...] + other[...] + extra).astype(BF16)


def final(shrunk, slot_column, factors, kept, other, owned):
    n, wide, share = factors.shape
    rows = kept.shape[0]
    return pl.pallas_call(
        functools.partial(final_kernel, n, owned),
        in_specs=[pl.BlockSpec(memory_space=pltpu.VMEM)] * 5,
        out_specs=pl.BlockSpec(memory_space=pltpu.VMEM),
        scratch_shapes=[pltpu.VMEM((rows, n * wide), BF16)],
        out_shape=jax.ShapeDtypeStruct((rows, share), BF16),
        compiler_params=params(40),
        cost_estimate=pl.CostEstimate(
            flops=2 * rows * share * n * wide,
            bytes_accessed=2 * n * wide * share + 10 * rows * share,
            transcendentals=0,
        ),
        name="expand_and_add",
    )(shrunk, slot_column, factors.reshape(n * wide, share), kept, other)


def make_shards(n, cores):
    order = ring_order(n)
    place_of = {store: place for place, store in enumerate(order)}
    clockwise = [(order[i], order[(i + 1) % n]) for i in range(n)]
    counter = [(order[i], order[i - 1]) for i in range(n)]
    long, short = n // 2, (n - 1) // 2
    swap = [(t, (t + 1) % cores) for t in range(cores)]
    hops = [[0] + [-i for i in range(1, a + 1)] + list(range(1, b + 1)) for a, b in ((long, short), (short, long))]
    table = np.array(
        [
            [order[(place_of[s] + hop) % n] for way in hops for hop in way] + [t, 1 - t]
            for s in range(n)
            for t in range(cores)
        ],
        np.int32,
    )
    half = 2 * n

    def shards(hidden, down, shrink, expand, row_adapter, adapter_slot):
        owned, units, rank = shrink.shape
        store, tensor = lax.axis_index("store"), lax.axis_index("tensor")
        scalars = lax.dynamic_slice_in_dim(jnp.asarray(table), store * cores + tensor, 1, 0)[0]
        shrink_rows = jnp.transpose(shrink, (0, 2, 1)).reshape(owned * rank, units)

        slots = jnp.arange(adapter_slot.shape[0], dtype=jnp.int32)
        row_slot = jnp.sum(jnp.where(row_adapter[None, :] == slots[:, None], adapter_slot[:, None], 0), axis=0)

        tiles = units // TILE
        large = (tiles + 2) // 4 * TILE
        small = (units - 2 * large) // (2 * TILE) * TILE
        widths = [units - 2 * large - small, large, large, small]

        acc = None
        start = 0
        after = {}
        blocks = expand_blocks(scalars, half, expand, n, cores)
        factors = lax.all_to_all(blocks, "store", 0, 0)
        for chunk, width in enumerate(widths):
            own = take(hidden, start, width, after[chunk]) if chunk in after else hidden[:, start:start + width]
            way = chunk % 2
            pieces = [own]
            for length, pairs in zip(((long, short), (short, long))[way], (clockwise, counter)):
                moving = own
                for step in range(length):
                    moving = lax.ppermute(moving, "store", pairs)
                    pieces.append(moving)
            if chunk == 0:
                after[2] = [pieces[(long, short)[way]], pieces[-1], blocks]
            if chunk == 1:
                after[3] = [pieces[(long, short)[way]], pieces[-1], factors]
            call = functools.partial(chunk_matmul, scalars, way * n, half, pieces, down, shrink_rows)
            if chunk < len(widths) - 1:
                acc = call(acc, start, (0, 1), True, f"chunk_{chunk}")
            else:
                narrow, = call(acc[2:], start, (), True, "last_narrow")
                mine = [
                    jnp.where((row_slot == store * owned + i)[None, :], narrow[i * rank:(i + 1) * rank], 0.0)
                    for i in range(owned)
                ]
                mine = sum(mine[1:], mine[0])
                send, = call(acc[1:2], start, (1,), False, "last_sent", [mine])
                kept, = call(acc[:1], start, (0,), False, "last_kept", [send])
            start += width
        shrunk = (mine + lax.ppermute(mine, "tensor", swap)).astype(BF16)
        other = lax.ppermute(send, "tensor", swap)
        bit = 1
        while bit < n:
            shrunk = shrunk + lax.ppermute(shrunk, "store", [(s, s ^ bit) for s in range(n)])
            bit *= 2
        return final(shrunk, row_slot[:, None], factors, kept, other, owned)

    return shards


def solution(mesh):
    in_specs = (
        P(("parts", "store"), "tensor"),
        P("tensor", "store"),
        P(("parts", "store"), "tensor", None),
        P(("parts", "store"), None, None),
        P("parts"),
        P("parts"),
    )
    out_specs = P("parts", ("store", "tensor"))
    shards = make_shards(mesh.shape["store"], mesh.shape["tensor"])
    return jax.shard_map(shards, mesh=mesh, in_specs=in_specs, out_specs=out_specs, check_vma=False)
```

```python
import functools

import jax
import jax.numpy as jnp
import numpy as np
from jax import lax
from jax.experimental import pallas as pl
from jax.experimental.pallas import tpu as pltpu
from jax.sharding import Mesh, PartitionSpec as P

F32, BF16 = jnp.float32, jnp.bfloat16
TILE = 1024
MIB = 2**20


def params(mib):
    return pltpu.CompilerParams(vmem_limit_bytes=mib * MIB)


def split_kernel(scalars, src, dst):
    dst[...] = src[...][None]


def expand_blocks(scalars, half, expand, n, cores):
    owned, rank, width = expand.shape
    rows = owned * rank
    share = width // (n * cores)
    return pl.pallas_call(
        split_kernel,
        grid_spec=pltpu.PrefetchScalarGridSpec(
            num_scalar_prefetch=1,
            grid=(n,),
            in_specs=[pl.BlockSpec((rows, share), lambda s, t: (0, s * cores + t[half]))],
            out_specs=pl.BlockSpec((1, rows, share), lambda s, t: (s, 0, 0)),
        ),
        out_shape=jax.ShapeDtypeStruct((n, rows, share), BF16),
        compiler_params=params(40),
        cost_estimate=pl.CostEstimate(flops=0, bytes_accessed=4 * n * rows * share, transcendentals=0),
        name="expand_blocks",
    )(scalars, expand.reshape(rows, width))


def matmul_kernel(count, waits, layout, sides, narrow, has_acc, scalars, *refs):
    refs = list(refs)[waits:]
    pieces = [refs.pop(0) for _ in range(count)]
    weights = [refs.pop(0) for _ in range(sides)]
    shrink = refs.pop(0) if narrow else None
    outs = sides + narrow
    before = [refs.pop(0) for _ in range(outs)] if has_acc else None
    after = [refs.pop(0) for _ in range(outs)]
    lhs, sems = refs
    step = pl.program_id(0)
    steps, all_rows, tile = lhs.shape
    rows = all_rows // len(layout)

    @pl.when(step == 0)
    def _():
        copies = []
        for i, (piece, block, pair, which) in enumerate(layout):
            at = pl.multiple_of((2 * pair + scalars[which]) * rows, rows)
            for j in range(steps):
                copies.append(
                    pltpu.make_async_copy(
                        pieces[piece].at[pl.ds(block * rows, rows), pl.ds(j * tile, tile)],
                        lhs.at[j, pl.ds(at, rows), :],
                        sems.at[i, j],
                    )
                )
        for copy in copies:
            copy.start()
        for i in range(outs):
            after[i][...] = before[i][...] if has_acc else jnp.zeros_like(after[i])
        for copy in copies:
            copy.wait()

    left = lhs[step]
    if narrow:
        after[-1][...] += lax.dot_general(
            shrink[...], left, (((1,), (1,)), ((), ())), preferred_element_type=F32
        )
    for i in range(sides):
        after[i][...] += jnp.dot(left, weights[i][...], preferred_element_type=F32)


def chunk_matmul(scalars, pieces, layout, down, shrink, acc, start, sides, narrow, label, after=()):
    rows, width = sum(piece.shape[0] for piece in pieces), pieces[0].shape[1]
    share = down.shape[1] // 2
    steps = width // TILE
    first = start // TILE
    ranks = shrink.shape[0]
    in_specs = [pl.BlockSpec(memory_space=pl.ANY) for _ in after]
    in_specs += [pl.BlockSpec(memory_space=pltpu.HBM) for _ in pieces]
    args = [*after, *pieces]
    for side in sides:
        in_specs.append(pl.BlockSpec((TILE, share), functools.partial(lambda side, k, s: (first + k, s[2 + side]), side)))
        args.append(down)
    if narrow:
        in_specs.append(pl.BlockSpec((ranks, TILE), lambda k, s: (0, first + k)))
        args.append(shrink)
    shapes = [(rows, share)] * len(sides) + [(ranks, rows)] * narrow
    whole = [pl.BlockSpec(shape, lambda k, s: (0, 0)) for shape in shapes]
    aliases = {}
    if acc is not None:
        aliases = {1 + len(args) + i: i for i in range(len(shapes))}
        in_specs += whole
        args += list(acc)
    columns = share * len(sides) + ranks * narrow
    return pl.pallas_call(
        functools.partial(matmul_kernel, len(pieces), len(after), layout, len(sides), narrow, acc is not None),
        grid_spec=pltpu.PrefetchScalarGridSpec(
            num_scalar_prefetch=1,
            grid=(steps,),
            in_specs=in_specs,
            out_specs=whole,
            scratch_shapes=[pltpu.VMEM((steps, rows, TILE), BF16), pltpu.SemaphoreType.DMA((len(layout), steps))],
        ),
        out_shape=[jax.ShapeDtypeStruct(shape, F32) for shape in shapes],
        input_output_aliases=aliases,
        compiler_params=params(40),
        cost_estimate=pl.CostEstimate(
            flops=4 * rows * width * columns,
            bytes_accessed=2 * width * (columns + rows) + 8 * rows * columns,
            transcendentals=0,
        ),
        name=label,
    )(scalars, *args)


def final_kernel(n, owned, shrunk, slot, factors, kept, other, out, spread):
    rank = shrunk.shape[0]
    wide = owned * rank
    rows = out.shape[0]
    lane = lax.broadcasted_iota(jnp.int32, (rows, wide), 1) // rank
    own = shrunk[...].astype(F32).T
    pair = jnp.concatenate([own] * owned, axis=1)
    place = slot[...] - lane
    for i in range(n):
        spread[:, i * wide:(i + 1) * wide] = jnp.where(place == i * owned, pair, 0.0).astype(BF16)
    extra = jnp.dot(spread[...], factors[...], preferred_element_type=F32)
    out[...] = (kept[...] + other[...] + extra).astype(BF16)


def final(shrunk, slot_column, factors, kept, other, owned):
    n, wide, share = factors.shape
    rows = kept.shape[0]
    return pl.pallas_call(
        functools.partial(final_kernel, n, owned),
        in_specs=[pl.BlockSpec(memory_space=pltpu.VMEM)] * 5,
        out_specs=pl.BlockSpec(memory_space=pltpu.VMEM),
        scratch_shapes=[pltpu.VMEM((rows, n * wide), BF16)],
        out_shape=jax.ShapeDtypeStruct((rows, share), BF16),
        compiler_params=params(40),
        cost_estimate=pl.CostEstimate(
            flops=2 * rows * share * n * wide,
            bytes_accessed=2 * n * wide * share + 10 * rows * share,
            transcendentals=0,
        ),
        name="expand_and_add",
    )(shrunk, slot_column, factors.reshape(n * wide, share), kept, other)


def make_shards(depth, cores):
    n = 2 * depth
    swap_y, swap_core = [(0, 1), (1, 0)], [(t, (t + 1) % cores) for t in range(cores)]
    table = np.array([[y, 1 - y, t, 1 - t] for y in range(2) for t in range(cores)], np.int32)
    gathered_first = tuple((piece, z, z, piece) for z in range(depth) for piece in range(2))

    def shards(hidden, down, shrink, expand, row_adapter, adapter_slot):
        owned, units, rank = shrink.shape
        y, tensor = lax.axis_index("y"), lax.axis_index("tensor")
        store = 2 * lax.axis_index("z") + y
        scalars = lax.dynamic_slice_in_dim(jnp.asarray(table), y * cores + tensor, 1, 0)[0]
        shrink_rows = jnp.transpose(shrink, (0, 2, 1)).reshape(owned * rank, units)

        slots = jnp.arange(adapter_slot.shape[0], dtype=jnp.int32)
        row_slot = jnp.sum(jnp.where(row_adapter[None, :] == slots[:, None], adapter_slot[:, None], 0), axis=0)

        tiles = units // TILE
        large = (tiles + 2) // 4 * TILE
        small = (units - 2 * large) // (2 * TILE) * TILE
        widths = [units - 2 * large - small, large, large, small]

        blocks = expand_blocks(scalars, 2, expand, n, cores)
        factors = lax.all_to_all(blocks, ("z", "y"), 0, 0)
        acc = None
        start = 0
        for chunk, width in enumerate(widths):
            column = lax.all_gather(hidden[:, start:start + width], "z", axis=0, tiled=True)
            pieces = [column, lax.ppermute(column, "y", swap_y)]
            call = functools.partial(chunk_matmul, scalars, pieces, gathered_first, down, shrink_rows)
            if chunk < len(widths) - 1:
                acc = call(acc, start, (0, 1), True, f"chunk_{chunk}")
            else:
                narrow, = call(acc[2:], start, (), True, "last_narrow")
                mine = [
                    jnp.where((row_slot == store * owned + i)[None, :], narrow[i * rank:(i + 1) * rank], 0.0)
                    for i in range(owned)
                ]
                mine = sum(mine[1:], mine[0])
                send, = call(acc[1:2], start, (1,), False, "last_sent", [mine])
                kept, = call(acc[:1], start, (0,), False, "last_kept", [send])
            start += width
        shrunk = (mine + lax.ppermute(mine, "tensor", swap_core)).astype(BF16)
        other = lax.ppermute(send, "tensor", swap_core)
        bit = 1
        while bit < n:
            shrunk = shrunk + lax.ppermute(shrunk, ("z", "y"), [(s, s ^ bit) for s in range(n)])
            bit *= 2
        return final(shrunk, row_slot[:, None], factors, kept, other, owned)

    return shards


def solution(mesh):
    parts, stores, cores = (mesh.shape[name] for name in ("parts", "store", "tensor"))
    split = Mesh(mesh.devices.reshape(parts, stores // 2, 2, cores), ("parts", "z", "y", "tensor"))
    in_specs = (
        P(("parts", "z", "y"), "tensor"),
        P("tensor", ("z", "y")),
        P(("parts", "z", "y"), "tensor", None),
        P(("parts", "z", "y"), None, None),
        P("parts"),
        P("parts"),
    )
    out_specs = P("parts", ("z", "y", "tensor"))
    shards = make_shards(stores // 2, cores)
    return jax.shard_map(shards, mesh=split, in_specs=in_specs, out_specs=out_specs, check_vma=False)
```

```python
import functools

import jax
import jax.numpy as jnp
import numpy as np
from jax import lax
from jax.experimental import pallas as pl
from jax.experimental.pallas import tpu as pltpu
from jax.sharding import PartitionSpec as P

F32, BF16 = jnp.float32, jnp.bfloat16
TILE = 1024
MIB = 2**20
MATMUL_MIB = 56


def params(mib):
    return pltpu.CompilerParams(vmem_limit_bytes=mib * MIB)


def ring_order(n):
    return list(range(0, n, 2)) + list(range(1, n, 2))[::-1]


def take_kernel(start, width, src, *refs):
    *_, dst, sem = refs
    copy = pltpu.make_async_copy(src.at[:, pl.ds(start, width)], dst, sem)
    copy.start()
    copy.wait()


def take(hidden, start, width, after):
    rows = hidden.shape[0]
    return pl.pallas_call(
        functools.partial(take_kernel, start, width),
        in_specs=[pl.BlockSpec(memory_space=pl.ANY)] * (1 + len(after)),
        out_specs=pl.BlockSpec(memory_space=pl.ANY),
        scratch_shapes=[pltpu.SemaphoreType.DMA],
        out_shape=jax.ShapeDtypeStruct((rows, width), BF16),
        compiler_params=params(40),
        cost_estimate=pl.CostEstimate(flops=0, bytes_accessed=4 * rows * width, transcendentals=0),
        name=f"take_{start}",
    )(hidden, *after)


def split_kernel(scalars, src, *refs):
    *_, dst, mark = refs
    dst[...] = src[...][None]
    mark[...] = jnp.zeros_like(mark)


def expand_blocks(scalars, half, expand, n, cores, after):
    owned, rank, width = expand.shape
    rows = owned * rank
    share = width // (n * cores)
    return pl.pallas_call(
        split_kernel,
        grid_spec=pltpu.PrefetchScalarGridSpec(
            num_scalar_prefetch=1,
            grid=(n,),
            in_specs=[pl.BlockSpec((rows, share), lambda s, t: (0, s * cores + t[half]))]
            + [pl.BlockSpec(memory_space=pl.ANY)] * len(after),
            out_specs=[pl.BlockSpec((1, rows, share), lambda s, t: (s, 0, 0)), pl.BlockSpec((8, 128), lambda s, t: (0, 0))],
        ),
        out_shape=[jax.ShapeDtypeStruct((n, rows, share), BF16), jax.ShapeDtypeStruct((8, 128), F32)],
        compiler_params=params(40),
        cost_estimate=pl.CostEstimate(flops=0, bytes_accessed=4 * n * rows * share, transcendentals=0),
        name="expand_blocks",
    )(scalars, expand.reshape(rows, width), *after)


def matmul_kernel(n, waits, base, sides, narrow, has_acc, token, scalars, *refs):
    refs = list(refs)[waits:]
    pieces = [refs.pop(0) for _ in range(n)]
    weights = [refs.pop(0) for _ in range(sides)]
    shrink = refs.pop(0) if narrow else None
    outs = sides + narrow
    before = [refs.pop(0) for _ in range(outs)] if has_acc else None
    acc = [refs.pop(0) for _ in range(outs)]
    if token:
        refs.pop(0)[...] = jnp.zeros((8, 128), F32)
    lhs, sems = refs
    step = pl.program_id(0)
    rows = pieces[0].shape[0]

    @pl.when(step == 0)
    def _():
        copies = []
        for i in range(n):
            at = pl.multiple_of(scalars[base + i] * rows, rows)
            copies.append(pltpu.make_async_copy(pieces[i], lhs.at[pl.ds(at, rows), :], sems.at[i]))
        for copy in copies:
            copy.start()
        for i, out in enumerate(acc):
            out[...] = before[i][...] if has_acc else jnp.zeros_like(out)
        for copy in copies:
            copy.wait()

    left = lhs[:, pl.ds(pl.multiple_of(step * TILE, TILE), TILE)]
    if narrow:
        acc[-1][...] += lax.dot_general(
            shrink[...], left, (((1,), (1,)), ((), ())), preferred_element_type=F32
        )
    for i in range(sides):
        acc[i][...] += jnp.dot(left, weights[i][...], preferred_element_type=F32)


def chunk_matmul(scalars, base, half, pieces, down, shrink, acc, start, sides, narrow, label, after=(), token=False):
    n = len(pieces)
    rows, width = pieces[0].shape[0] * n, pieces[0].shape[1]
    share = down.shape[1] // 2
    steps = width // TILE
    first = start // TILE
    ranks = shrink.shape[0]
    in_specs = [pl.BlockSpec(memory_space=pl.ANY) for _ in after]
    in_specs += [pl.BlockSpec(memory_space=pltpu.HBM) for _ in pieces]
    args = [*after, *pieces]
    for side in sides:
        in_specs.append(pl.BlockSpec((TILE, share), functools.partial(lambda side, k, s: (first + k, s[half + side]), side)))
        args.append(down)
    if narrow:
        in_specs.append(pl.BlockSpec((ranks, TILE), lambda k, s: (0, first + k)))
        args.append(shrink)
    shapes = [(rows, share)] * len(sides) + [(ranks, rows)] * narrow
    whole = [pl.BlockSpec(shape, lambda k, s: (0, 0)) for shape in shapes]
    aliases = {}
    if acc is not None:
        aliases = {1 + len(args) + i: i for i in range(len(shapes))}
        in_specs += whole
        args += list(acc)
    columns = share * len(sides) + ranks * narrow
    marks = [(8, 128)] * token
    return pl.pallas_call(
        functools.partial(matmul_kernel, n, len(after), base, len(sides), narrow, acc is not None, token),
        grid_spec=pltpu.PrefetchScalarGridSpec(
            num_scalar_prefetch=1,
            grid=(steps,),
            in_specs=in_specs,
            out_specs=whole + [pl.BlockSpec((8, 128), lambda k, s: (0, 0))] * token,
            scratch_shapes=[pltpu.VMEM((rows, width), BF16), pltpu.SemaphoreType.DMA((n,))],
        ),
        out_shape=[jax.ShapeDtypeStruct(shape, F32) for shape in shapes + marks],
        input_output_aliases=aliases,
        compiler_params=params(MATMUL_MIB),
        cost_estimate=pl.CostEstimate(
            flops=4 * rows * width * columns,
            bytes_accessed=2 * width * (columns + rows) + 8 * rows * columns,
            transcendentals=0,
        ),
        name=label,
    )(scalars, *args)


def final_kernel(n, owned, shrunk, slot, factors, kept, other, out, spread):
    rank = shrunk.shape[0]
    wide = owned * rank
    rows = out.shape[0]
    lane = lax.broadcasted_iota(jnp.int32, (rows, wide), 1) // rank
    own = shrunk[...].astype(F32).T
    pair = jnp.concatenate([own] * owned, axis=1)
    place = slot[...] - lane
    for i in range(n):
        spread[:, i * wide:(i + 1) * wide] = jnp.where(place == i * owned, pair, 0.0).astype(BF16)
    extra = jnp.dot(spread[...], factors[...], preferred_element_type=F32)
    out[...] = (kept[...] + other[...] + extra).astype(BF16)


def final(shrunk, slot_column, factors, kept, other, owned):
    n, wide, share = factors.shape
    rows = kept.shape[0]
    return pl.pallas_call(
        functools.partial(final_kernel, n, owned),
        in_specs=[pl.BlockSpec(memory_space=pltpu.VMEM)] * 5,
        out_specs=pl.BlockSpec(memory_space=pltpu.VMEM),
        scratch_shapes=[pltpu.VMEM((rows, n * wide), BF16)],
        out_shape=jax.ShapeDtypeStruct((rows, share), BF16),
        compiler_params=params(40),
        cost_estimate=pl.CostEstimate(
            flops=2 * rows * share * n * wide,
            bytes_accessed=2 * n * wide * share + 10 * rows * share,
            transcendentals=0,
        ),
        name="expand_and_add",
    )(shrunk, slot_column, factors.reshape(n * wide, share), kept, other)


def make_shards(n, cores):
    order = ring_order(n)
    place_of = {store: place for place, store in enumerate(order)}
    clockwise = [(order[i], order[(i + 1) % n]) for i in range(n)]
    counter = [(order[i], order[i - 1]) for i in range(n)]
    long, short = n // 2, (n - 1) // 2
    swap = [(t, (t + 1) % cores) for t in range(cores)]
    hops = [[0] + [-i for i in range(1, a + 1)] + list(range(1, b + 1)) for a, b in ((long, short), (short, long))]
    table = np.array(
        [
            [order[(place_of[s] + hop) % n] for way in hops for hop in way] + [t, 1 - t]
            for s in range(n)
            for t in range(cores)
        ],
        np.int32,
    )
    half = 2 * n

    def shards(hidden, down, shrink, expand, row_adapter, adapter_slot):
        owned, units, rank = shrink.shape
        store, tensor = lax.axis_index("store"), lax.axis_index("tensor")
        scalars = lax.dynamic_slice_in_dim(jnp.asarray(table), store * cores + tensor, 1, 0)[0]
        shrink_rows = jnp.transpose(shrink, (0, 2, 1)).reshape(owned * rank, units)

        slots = jnp.arange(adapter_slot.shape[0], dtype=jnp.int32)
        row_slot = jnp.sum(jnp.where(row_adapter[None, :] == slots[:, None], adapter_slot[:, None], 0), axis=0)

        tiles = units // TILE
        large = (tiles + 2) // 4 * TILE
        small = (units - 2 * large) // (2 * TILE) * TILE
        widths = [units - 2 * large - small, large, large, small]

        acc = None
        start = 0
        after = {}
        for chunk, width in enumerate(widths):
            own = take(hidden, start, width, after[chunk]) if chunk in after else hidden[:, start:start + width]
            way = chunk % 2
            pieces = [own]
            lengths = ((long, short), (short, long))[way]
            for length, pairs in zip(lengths, (clockwise, counter)):
                moving = own
                for step in range(length):
                    moving = lax.ppermute(moving, "store", pairs)
                    pieces.append(moving)
            call = functools.partial(chunk_matmul, scalars, way * n, half, pieces, down, shrink_rows)
            if chunk < len(widths) - 1:
                ends, late = [pieces[lengths[0]], pieces[-1]], [pieces[lengths[0] - 1], pieces[-2]]
                first = []
                if chunk == 2:
                    blocks, *first = expand_blocks(scalars, half, expand, n, cores, [*late, token])
                    factors = lax.all_to_all(blocks, "store", 0, 0)
                *acc, token = call(acc, start, (0, 1), True, f"chunk_{chunk}", first, True)
                if chunk == 0:
                    after[2], after[3] = ends, [token]
                if chunk == 1:
                    after[3] += ends
            else:
                narrow, = call(acc[2:], start, (), True, "last_narrow")
                mine = [
                    jnp.where((row_slot == store * owned + i)[None, :], narrow[i * rank:(i + 1) * rank], 0.0)
                    for i in range(owned)
                ]
                mine = sum(mine[1:], mine[0])
                send, = call(acc[1:2], start, (1,), False, "last_sent", [mine])
                kept, = call(acc[:1], start, (0,), False, "last_kept", [send])
            start += width
        shrunk = (mine + lax.ppermute(mine, "tensor", swap)).astype(BF16)
        other = lax.ppermute(send, "tensor", swap)
        bit = 1
        while bit < n:
            shrunk = shrunk + lax.ppermute(shrunk, "store", [(s, s ^ bit) for s in range(n)])
            bit *= 2
        return final(shrunk, row_slot[:, None], factors, kept, other, owned)

    return shards


def solution(mesh):
    in_specs = (
        P(("parts", "store"), "tensor"),
        P("tensor", "store"),
        P(("parts", "store"), "tensor", None),
        P(("parts", "store"), None, None),
        P("parts"),
        P("parts"),
    )
    out_specs = P("parts", ("store", "tensor"))
    shards = make_shards(mesh.shape["store"], mesh.shape["tensor"])
    return jax.shard_map(shards, mesh=mesh, in_specs=in_specs, out_specs=out_specs, check_vma=False)
```

```python
import functools

import jax
import jax.numpy as jnp
import numpy as np
from jax import lax
from jax.experimental import pallas as pl
from jax.experimental.pallas import tpu as pltpu
from jax.sharding import PartitionSpec as P

F32, BF16 = jnp.float32, jnp.bfloat16
TILE = 1024
MIB = 2**20
MATMUL_MIB = 48


def params(mib):
    return pltpu.CompilerParams(vmem_limit_bytes=mib * MIB)


def ring_order(n):
    return list(range(0, n, 2)) + list(range(1, n, 2))[::-1]


def take_kernel(start, width, src, *refs):
    *_, dst, sem = refs
    copy = pltpu.make_async_copy(src.at[:, pl.ds(start, width)], dst, sem)
    copy.start()
    copy.wait()


def take(hidden, start, width, after):
    rows = hidden.shape[0]
    return pl.pallas_call(
        functools.partial(take_kernel, start, width),
        in_specs=[pl.BlockSpec(memory_space=pl.ANY)] * (1 + len(after)),
        out_specs=pl.BlockSpec(memory_space=pl.ANY),
        scratch_shapes=[pltpu.SemaphoreType.DMA],
        out_shape=jax.ShapeDtypeStruct((rows, width), BF16),
        compiler_params=params(MATMUL_MIB),
        cost_estimate=pl.CostEstimate(flops=0, bytes_accessed=4 * rows * width, transcendentals=0),
        name=f"take_{start}",
    )(hidden, *after)


def split_kernel(scalars, src, dst):
    dst[...] = src[...][None]


def expand_blocks(scalars, half, expand, n, cores):
    owned, rank, width = expand.shape
    rows = owned * rank
    share = width // (n * cores)
    return pl.pallas_call(
        split_kernel,
        grid_spec=pltpu.PrefetchScalarGridSpec(
            num_scalar_prefetch=1,
            grid=(n,),
            in_specs=[pl.BlockSpec((rows, share), lambda s, t: (0, s * cores + t[half]))],
            out_specs=pl.BlockSpec((1, rows, share), lambda s, t: (s, 0, 0)),
        ),
        out_shape=jax.ShapeDtypeStruct((n, rows, share), BF16),
        compiler_params=params(MATMUL_MIB),
        cost_estimate=pl.CostEstimate(flops=0, bytes_accessed=4 * n * rows * share, transcendentals=0),
        name="expand_blocks",
    )(scalars, expand.reshape(rows, width))


def tie_kernel(*refs):
    pass


def tie(array, after):
    return pl.pallas_call(
        tie_kernel,
        in_specs=[pl.BlockSpec(memory_space=pl.ANY)] * (1 + len(after)),
        out_specs=pl.BlockSpec(memory_space=pl.ANY),
        out_shape=jax.ShapeDtypeStruct(array.shape, array.dtype),
        input_output_aliases={0: 0},
        compiler_params=params(MATMUL_MIB),
        name="tie",
    )(array, *after)


def matmul_kernel(n, waits, base, half, start, tiles, sides, narrow, has_acc, token, scalars, *refs):
    refs = list(refs)[waits:]
    pieces = [refs.pop(0) for _ in range(n)]
    down = refs.pop(0)
    shrink = refs.pop(0)
    outs = len(sides) + narrow
    before = [refs.pop(0) for _ in range(outs)] if has_acc else []
    acc = [refs.pop(0) for _ in range(outs)]
    if token:
        refs.pop(0)[...] = jnp.zeros((8, 128), F32)
    lefts = [refs.pop(0) for _ in tiles]
    weights = [[refs.pop(0) for _ in tiles] for _ in sides]
    ranks = [refs.pop(0) for _ in tiles] if narrow else []
    earlier = [refs.pop(0) for _ in before]
    sems, old_sems = refs
    rows = pieces[0].shape[0]
    share = down.shape[1] // 2

    copies = []
    at = 0
    for k, tile in enumerate(tiles):
        group = []
        for i in range(n):
            to = pl.multiple_of(scalars[base + i] * rows, rows)
            group.append((pieces[i].at[:, pl.ds(at, tile)], lefts[k].at[pl.ds(to, rows), :]))
        if narrow:
            group.append((shrink.at[:, pl.ds(start + at, tile)], ranks[k]))
        for i, side in enumerate(sides):
            column = pl.multiple_of(scalars[half + side] * share, share)
            group.append((down.at[pl.ds(start + at, tile), pl.ds(column, share)], weights[i][k]))
        copies.append([pltpu.make_async_copy(*pair, sems.at[k, i]) for i, pair in enumerate(group)])
        for copy in copies[-1]:
            copy.start()
        at += tile
    old = [pltpu.make_async_copy(a, b, old_sems.at[i]) for i, (a, b) in enumerate(zip(before, earlier))]
    for copy in old:
        copy.start()

    for k in range(len(tiles)):
        for copy in copies[k]:
            copy.wait()
        left = lefts[k][...]
        terms = [jnp.dot(left, weights[i][k][...], preferred_element_type=F32) for i in range(len(sides))]
        if narrow:
            terms.append(
                lax.dot_general(ranks[k][...], left, (((1,), (1,)), ((), ())), preferred_element_type=F32)
            )
        for i, term in enumerate(terms):
            acc[i][...] = term if k == 0 else acc[i][...] + term
    for i, copy in enumerate(old):
        copy.wait()
        acc[i][...] += earlier[i][...]


def chunk_matmul(scalars, base, half, pieces, down, shrink, acc, start, sides, narrow, label, after=(), token=False):
    n = len(pieces)
    rows, width = pieces[0].shape[0] * n, pieces[0].shape[1]
    share = down.shape[1] // 2
    ranks = shrink.shape[0]
    tiles = [TILE // 2] * 2 + [TILE] * (width // TILE - 1)
    anywhere = pl.BlockSpec(memory_space=pl.ANY)
    args = [*after, *pieces, down, shrink, *(acc or ())]
    shapes = [(rows, share)] * len(sides) + [(ranks, rows)] * narrow
    columns = share * len(sides) + ranks * narrow
    marks = [(8, 128)] * token
    return pl.pallas_call(
        functools.partial(
            matmul_kernel, n, len(after), base, half, start, tiles, sides, narrow, acc is not None, token
        ),
        grid_spec=pltpu.PrefetchScalarGridSpec(
            num_scalar_prefetch=1,
            grid=(),
            in_specs=[anywhere] * len(args),
            out_specs=[pl.BlockSpec(memory_space=pltpu.VMEM)] * len(shapes + marks),
            scratch_shapes=[pltpu.VMEM((rows, tile), BF16) for tile in tiles]
            + [pltpu.VMEM((tile, share), BF16) for _ in sides for tile in tiles]
            + [pltpu.VMEM((ranks, tile), BF16) for tile in tiles if narrow]
            + [pltpu.VMEM(shape, F32) for shape in shapes if acc is not None]
            + [pltpu.SemaphoreType.DMA((len(tiles), n + 3)), pltpu.SemaphoreType.DMA((3,))],
        ),
        out_shape=[jax.ShapeDtypeStruct(shape, F32) for shape in shapes + marks],
        compiler_params=params(MATMUL_MIB),
        cost_estimate=pl.CostEstimate(
            flops=4 * rows * width * columns,
            bytes_accessed=2 * width * (columns + rows) + 8 * rows * columns,
            transcendentals=0,
        ),
        name=label,
    )(scalars, *args)


def final_kernel(n, owned, shrunk, slot, factors, kept, other, out, spread):
    rank = shrunk.shape[0]
    wide = owned * rank
    rows = out.shape[0]
    lane = lax.broadcasted_iota(jnp.int32, (rows, wide), 1) // rank
    own = shrunk[...].astype(F32).T
    pair = jnp.concatenate([own] * owned, axis=1)
    place = slot[...] - lane
    for i in range(n):
        spread[:, i * wide:(i + 1) * wide] = jnp.where(place == i * owned, pair, 0.0).astype(BF16)
    extra = jnp.dot(spread[...], factors[...], preferred_element_type=F32)
    out[...] = (kept[...] + other[...] + extra).astype(BF16)


def final(shrunk, slot_column, factors, kept, other, owned):
    n, wide, share = factors.shape
    rows = kept.shape[0]
    return pl.pallas_call(
        functools.partial(final_kernel, n, owned),
        in_specs=[pl.BlockSpec(memory_space=pltpu.VMEM)] * 5,
        out_specs=pl.BlockSpec(memory_space=pltpu.VMEM),
        scratch_shapes=[pltpu.VMEM((rows, n * wide), BF16)],
        out_shape=jax.ShapeDtypeStruct((rows, share), BF16),
        compiler_params=params(MATMUL_MIB),
        cost_estimate=pl.CostEstimate(
            flops=2 * rows * share * n * wide,
            bytes_accessed=2 * n * wide * share + 10 * rows * share,
            transcendentals=0,
        ),
        name="expand_and_add",
    )(shrunk, slot_column, factors.reshape(n * wide, share), kept, other)


def make_shards(n, cores):
    order = ring_order(n)
    place_of = {store: place for place, store in enumerate(order)}
    clockwise = [(order[i], order[(i + 1) % n]) for i in range(n)]
    counter = [(order[i], order[i - 1]) for i in range(n)]
    long, short = n // 2, (n - 1) // 2
    swap = [(t, (t + 1) % cores) for t in range(cores)]
    hops = [[0] + [-i for i in range(1, a + 1)] + list(range(1, b + 1)) for a, b in ((long, short), (short, long))]
    table = np.array(
        [
            [order[(place_of[s] + hop) % n] for way in hops for hop in way] + [t, 1 - t]
            for s in range(n)
            for t in range(cores)
        ],
        np.int32,
    )
    half = 2 * n

    def shards(hidden, down, shrink, expand, row_adapter, adapter_slot):
        owned, units, rank = shrink.shape
        store, tensor = lax.axis_index("store"), lax.axis_index("tensor")
        scalars = lax.dynamic_slice_in_dim(jnp.asarray(table), store * cores + tensor, 1, 0)[0]
        shrink_rows = jnp.transpose(shrink, (0, 2, 1)).reshape(owned * rank, units)

        slots = jnp.arange(adapter_slot.shape[0], dtype=jnp.int32)
        row_slot = jnp.sum(jnp.where(row_adapter[None, :] == slots[:, None], adapter_slot[:, None], 0), axis=0)

        large = 2 * (units // (7 * TILE)) * TILE
        widths = [units - 3 * large, large, large, large]

        blocks = expand_blocks(scalars, half, expand, n, cores)
        acc = None
        start = 0
        after = {}
        for chunk, width in enumerate(widths):
            own = take(hidden, start, width, after[chunk]) if chunk in after else hidden[:, start:start + width]
            way = chunk % 2
            pieces = [own]
            lengths = ((long, short), (short, long))[way]
            for length, pairs in zip(lengths, (clockwise, counter)):
                moving = own
                for step in range(length):
                    moving = lax.ppermute(moving, "store", pairs)
                    pieces.append(moving)
            ends = [pieces[lengths[0]], pieces[-1]]
            call = functools.partial(chunk_matmul, scalars, way * n, half, pieces, down, shrink_rows)
            if chunk < len(widths) - 1:
                *acc, token = call(acc, start, (0, 1), True, f"chunk_{chunk}", token=True)
                if chunk == 0:
                    after[3] = ends
            else:
                factors = lax.all_to_all(tie(blocks, ends), "store", 0, 0)
                narrow, = call(acc[2:], start, (), True, "last_narrow")
                mine = [
                    jnp.where((row_slot == store * owned + i)[None, :], narrow[i * rank:(i + 1) * rank], 0.0)
                    for i in range(owned)
                ]
                mine = sum(mine[1:], mine[0])
                send, = call(acc[1:2], start, (1,), False, "last_sent", [mine])
                kept, = call(acc[:1], start, (0,), False, "last_kept", [send])
            start += width
        where = [(s, t) for s in range(n) for t in range(cores)]
        whole = mine
        for ds in range(2):
            for dt in range(cores):
                if ds or dt:
                    pairs = [(s * cores + t, (s ^ ds) * cores + (t + dt) % cores) for s, t in where]
                    whole = whole + lax.ppermute(mine, ("store", "tensor"), pairs)
        column = whole.astype(BF16)
        shrunk = column
        for ds in range(2, n, 2):
            shrunk = shrunk + lax.ppermute(column, "store", [(s, (s + ds) % n) for s in range(n)])
        other = lax.ppermute(send, "tensor", swap)
        return final(shrunk, row_slot[:, None], factors, kept, other, owned)

    return shards


def solution(mesh):
    in_specs = (
        P(("parts", "store"), "tensor"),
        P("tensor", "store"),
        P(("parts", "store"), "tensor", None),
        P(("parts", "store"), None, None),
        P("parts"),
        P("parts"),
    )
    out_specs = P("parts", ("store", "tensor"))
    shards = make_shards(mesh.shape["store"], mesh.shape["tensor"])
    return jax.shard_map(shards, mesh=mesh, in_specs=in_specs, out_specs=out_specs, check_vma=False)
```

```python
import functools

import jax
import jax.numpy as jnp
import numpy as np
from jax import lax
from jax.experimental import pallas as pl
from jax.experimental.pallas import tpu as pltpu
from jax.sharding import PartitionSpec as P

F32, BF16 = jnp.float32, jnp.bfloat16
TILE = 1024
CHUNKS = 4
MIB = 2**20
MATMUL_MIB = 62


def params(mib):
    return pltpu.CompilerParams(vmem_limit_bytes=mib * MIB)


def ring_order(n):
    return list(range(0, n, 2)) + list(range(1, n, 2))[::-1]


def take_kernel(start, width, src, *refs):
    *_, dst, sem = refs
    copy = pltpu.make_async_copy(src.at[:, pl.ds(start, width)], dst, sem)
    copy.start()
    copy.wait()


def take(hidden, start, width, after):
    rows = hidden.shape[0]
    return pl.pallas_call(
        functools.partial(take_kernel, start, width),
        in_specs=[pl.BlockSpec(memory_space=pl.ANY)] * (1 + len(after)),
        out_specs=pl.BlockSpec(memory_space=pl.ANY),
        scratch_shapes=[pltpu.SemaphoreType.DMA],
        out_shape=jax.ShapeDtypeStruct((rows, width), BF16),
        compiler_params=params(MATMUL_MIB),
        cost_estimate=pl.CostEstimate(flops=0, bytes_accessed=4 * rows * width, transcendentals=0),
        name=f"take_{start}",
    )(hidden, *after)


def split_kernel(scalars, src, dst, mark):
    dst[...] = src[...][None]
    mark[...] = jnp.zeros_like(mark)


def expand_blocks(scalars, half, expand, n, cores):
    owned, rank, width = expand.shape
    rows = owned * rank
    share = width // (n * cores)
    return pl.pallas_call(
        split_kernel,
        grid_spec=pltpu.PrefetchScalarGridSpec(
            num_scalar_prefetch=1,
            grid=(n,),
            in_specs=[pl.BlockSpec((rows, share), lambda s, t: (0, s * cores + t[half]))],
            out_specs=[pl.BlockSpec((1, rows, share), lambda s, t: (s, 0, 0)), pl.BlockSpec((8, 128), lambda s, t: (0, 0))],
        ),
        out_shape=[jax.ShapeDtypeStruct((n, rows, share), BF16), jax.ShapeDtypeStruct((8, 128), F32)],
        compiler_params=params(MATMUL_MIB),
        cost_estimate=pl.CostEstimate(flops=0, bytes_accessed=4 * n * rows * share, transcendentals=0),
        name="expand_blocks",
    )(scalars, expand.reshape(rows, width))


def tie_kernel(*refs):
    pass


def tie(array, after):
    return pl.pallas_call(
        tie_kernel,
        in_specs=[pl.BlockSpec(memory_space=pl.ANY)] * (1 + len(after)),
        out_specs=pl.BlockSpec(memory_space=pl.ANY),
        out_shape=jax.ShapeDtypeStruct(array.shape, array.dtype),
        input_output_aliases={0: 0},
        compiler_params=params(MATMUL_MIB),
        name="tie",
    )(array, *after)


def matmul_kernel(n, waits, spans, half, sides, narrow, has_acc, scalars, *refs):
    refs = list(refs)[waits:]
    pieces = [[refs.pop(0) for _ in range(n)] for _ in spans]
    down = refs.pop(0)
    shrink = refs.pop(0)
    outs = len(sides) + narrow
    before = [refs.pop(0) for _ in range(outs)] if has_acc else []
    acc = [refs.pop(0) for _ in range(outs)]
    tiles = [(part, at, tile) for part, (_, _, cuts) in enumerate(spans) for at, tile in cuts]
    lefts = [refs.pop(0) for _ in tiles]
    weights = [[refs.pop(0) for _ in tiles] for _ in sides]
    ranks = [refs.pop(0) for _ in tiles] if narrow else []
    earlier = [refs.pop(0) for _ in before]
    sems, old_sems = refs
    rows = pieces[0][0].shape[0]
    share = down.shape[1] // 2

    copies = []
    for k, (part, at, tile) in enumerate(tiles):
        base, start, _ = spans[part]
        group = []
        for i in range(n):
            to = pl.multiple_of(scalars[base + i] * rows, rows)
            group.append((pieces[part][i].at[:, pl.ds(at, tile)], lefts[k].at[pl.ds(to, rows), :]))
        if narrow:
            group.append((shrink.at[:, pl.ds(start + at, tile)], ranks[k]))
        for i, side in enumerate(sides):
            column = pl.multiple_of(scalars[half + side] * share, share)
            group.append((down.at[pl.ds(start + at, tile), pl.ds(column, share)], weights[i][k]))
        copies.append([pltpu.make_async_copy(*pair, sems.at[k, i]) for i, pair in enumerate(group)])
        for copy in copies[-1]:
            copy.start()
    old = [pltpu.make_async_copy(a, b, old_sems.at[i]) for i, (a, b) in enumerate(zip(before, earlier))]
    for copy in old:
        copy.start()

    for k in range(len(tiles)):
        for copy in copies[k]:
            copy.wait()
        left = lefts[k][...]
        terms = [jnp.dot(left, weights[i][k][...], preferred_element_type=F32) for i in range(len(sides))]
        if narrow:
            terms.append(
                lax.dot_general(ranks[k][...], left, (((1,), (1,)), ((), ())), preferred_element_type=F32)
            )
        for i, term in enumerate(terms):
            acc[i][...] = term if k == 0 else acc[i][...] + term
    for i, copy in enumerate(old):
        copy.wait()
        acc[i][...] += earlier[i][...]


def cuts_of(width):
    first = width % TILE or TILE
    sizes = [first // 2] * 2 if first == TILE else [first]
    sizes += [TILE] * ((width - first) // TILE)
    return [(sum(sizes[:i]), size) for i, size in enumerate(sizes)]


def chunk_matmul(scalars, half, chunks, down, shrink, acc, sides, narrow, label, after=()):
    n = len(chunks[0][0])
    rows = chunks[0][0][0].shape[0] * n
    share = down.shape[1] // 2
    ranks = shrink.shape[0]
    spans = [(base, start, cuts_of(pieces[0].shape[1])) for pieces, base, start in chunks]
    sizes = [tile for _, _, cuts in spans for _, tile in cuts]
    width = sum(sizes)
    anywhere = pl.BlockSpec(memory_space=pl.ANY)
    args = [*after, *(piece for pieces, _, _ in chunks for piece in pieces), down, shrink, *(acc or ())]
    shapes = [(rows, share)] * len(sides) + [(ranks, rows)] * narrow
    columns = share * len(sides) + ranks * narrow
    return pl.pallas_call(
        functools.partial(matmul_kernel, n, len(after), spans, half, sides, narrow, acc is not None),
        grid_spec=pltpu.PrefetchScalarGridSpec(
            num_scalar_prefetch=1,
            grid=(),
            in_specs=[anywhere] * len(args),
            out_specs=[pl.BlockSpec(memory_space=pltpu.VMEM)] * len(shapes),
            scratch_shapes=[pltpu.VMEM((rows, tile), BF16) for tile in sizes]
            + [pltpu.VMEM((tile, share), BF16) for _ in sides for tile in sizes]
            + [pltpu.VMEM((ranks, tile), BF16) for tile in sizes if narrow]
            + [pltpu.VMEM(shape, F32) for shape in shapes if acc is not None]
            + [pltpu.SemaphoreType.DMA((len(sizes), n + 3)), pltpu.SemaphoreType.DMA((3,))],
        ),
        out_shape=[jax.ShapeDtypeStruct(shape, F32) for shape in shapes],
        compiler_params=params(MATMUL_MIB),
        cost_estimate=pl.CostEstimate(
            flops=4 * rows * width * columns,
            bytes_accessed=2 * width * (columns + rows) + 8 * rows * columns,
            transcendentals=0,
        ),
        name=label,
    )(scalars, *args)


def final_kernel(n, owned, shrunk, slot, factors, kept, other, out, spread):
    rank = shrunk.shape[0]
    wide = owned * rank
    rows = out.shape[0]
    lane = lax.broadcasted_iota(jnp.int32, (rows, wide), 1) // rank
    own = shrunk[...].astype(F32).T
    pair = jnp.concatenate([own] * owned, axis=1)
    place = slot[...] - lane
    for i in range(n):
        spread[:, i * wide:(i + 1) * wide] = jnp.where(place == i * owned, pair, 0.0).astype(BF16)
    extra = jnp.dot(spread[...], factors[...], preferred_element_type=F32)
    out[...] = (kept[...] + other[...] + extra).astype(BF16)


def final(shrunk, slot_column, factors, kept, other, owned):
    n, wide, share = factors.shape
    rows = kept.shape[0]
    return pl.pallas_call(
        functools.partial(final_kernel, n, owned),
        in_specs=[pl.BlockSpec(memory_space=pltpu.VMEM)] * 5,
        out_specs=pl.BlockSpec(memory_space=pltpu.VMEM),
        scratch_shapes=[pltpu.VMEM((rows, n * wide), BF16)],
        out_shape=jax.ShapeDtypeStruct((rows, share), BF16),
        compiler_params=params(MATMUL_MIB),
        cost_estimate=pl.CostEstimate(
            flops=2 * rows * share * n * wide,
            bytes_accessed=2 * n * wide * share + 10 * rows * share,
            transcendentals=0,
        ),
        name="expand_and_add",
    )(shrunk, slot_column, factors.reshape(n * wide, share), kept, other)


def make_shards(n, cores):
    order = ring_order(n)
    place_of = {store: place for place, store in enumerate(order)}
    clockwise = [(order[i], order[(i + 1) % n]) for i in range(n)]
    counter = [(order[i], order[i - 1]) for i in range(n)]
    long, short = n // 2, (n - 1) // 2
    swap = [(t, (t + 1) % cores) for t in range(cores)]
    hops = [[0] + [-i for i in range(1, a + 1)] + list(range(1, b + 1)) for a, b in ((long, short), (short, long))]
    table = np.array(
        [
            [order[(place_of[s] + hop) % n] for way in hops for hop in way] + [t, 1 - t]
            for s in range(n)
            for t in range(cores)
        ],
        np.int32,
    )
    half = 2 * n

    def shards(hidden, down, shrink, expand, row_adapter, adapter_slot):
        owned, units, rank = shrink.shape
        store, tensor = lax.axis_index("store"), lax.axis_index("tensor")
        scalars = lax.dynamic_slice_in_dim(jnp.asarray(table), store * cores + tensor, 1, 0)[0]
        shrink_rows = jnp.transpose(shrink, (0, 2, 1)).reshape(owned * rank, units)

        slots = jnp.arange(adapter_slot.shape[0], dtype=jnp.int32)
        row_slot = jnp.sum(jnp.where(row_adapter[None, :] == slots[:, None], adapter_slot[:, None], 0), axis=0)

        width = units // CHUNKS
        blocks, mark = expand_blocks(scalars, half, expand, n, cores)
        chunks, ends = [], []
        for chunk in range(CHUNKS):
            start = chunk * width
            own = take(hidden, start, width, [mark]) if chunk == CHUNKS - 1 else hidden[:, start:start + width]
            way = chunk % 2
            pieces = [own]
            for length, pairs in zip(((long, short), (short, long))[way], (clockwise, counter)):
                moving = own
                for step in range(length):
                    moving = lax.ppermute(moving, "store", pairs)
                    pieces.append(moving)
                ends.append(moving)
            chunks.append((pieces, way * n, start))
        factors = lax.all_to_all(tie(blocks, ends[:4]), "store", 0, 0)

        call = functools.partial(chunk_matmul, scalars, half)
        acc = None
        for chunk in range(CHUNKS - 2):
            acc = call(chunks[chunk:chunk + 1], down, shrink_rows, acc, (0, 1), True, f"chunk_{chunk}")
        last = chunks[CHUNKS - 2:]
        narrow, = call(last, down, shrink_rows, acc[2:], (), True, "last_narrow")
        mine = [
            jnp.where((row_slot == store * owned + i)[None, :], narrow[i * rank:(i + 1) * rank], 0.0)
            for i in range(owned)
        ]
        mine = sum(mine[1:], mine[0])
        send, = call(last, down, shrink_rows, acc[1:2], (1,), False, "last_sent", [mine])
        kept, = call(last, down, shrink_rows, acc[:1], (0,), False, "last_kept", [send])
        where = [(s, t) for s in range(n) for t in range(cores)]
        whole = mine
        for ds in range(2):
            for dt in range(cores):
                if ds or dt:
                    pairs = [(s * cores + t, (s ^ ds) * cores + (t + dt) % cores) for s, t in where]
                    whole = whole + lax.ppermute(mine, ("store", "tensor"), pairs)
        column = whole.astype(BF16)
        shrunk = column
        for ds in range(2, n, 2):
            shrunk = shrunk + lax.ppermute(column, "store", [(s, (s + ds) % n) for s in range(n)])
        other = lax.ppermute(send, "tensor", swap)
        return final(shrunk, row_slot[:, None], factors, kept, other, owned)

    return shards


def solution(mesh):
    in_specs = (
        P(("parts", "store"), "tensor"),
        P("tensor", "store"),
        P(("parts", "store"), "tensor", None),
        P(("parts", "store"), None, None),
        P("parts"),
        P("parts"),
    )
    out_specs = P("parts", ("store", "tensor"))
    shards = make_shards(mesh.shape["store"], mesh.shape["tensor"])
    return jax.shard_map(shards, mesh=mesh, in_specs=in_specs, out_specs=out_specs, check_vma=False)
```

```python
import functools

import jax
import jax.numpy as jnp
import numpy as np
from jax import lax
from jax.experimental import pallas as pl
from jax.experimental.pallas import tpu as pltpu
from jax.sharding import PartitionSpec as P

F32, BF16 = jnp.float32, jnp.bfloat16
TILE = 2048
MIB = 2**20
MATMUL_MIB = 62


def params(mib):
    return pltpu.CompilerParams(vmem_limit_bytes=mib * MIB)


def ring_order(n):
    return list(range(0, n, 2)) + list(range(1, n, 2))[::-1]


def split_kernel(scalars, src, dst, mark):
    dst[...] = src[...][None]
    mark[...] = jnp.zeros_like(mark)


def expand_blocks(scalars, half, expand, n, cores):
    owned, rank, width = expand.shape
    rows = owned * rank
    share = width // (n * cores)
    return pl.pallas_call(
        split_kernel,
        grid_spec=pltpu.PrefetchScalarGridSpec(
            num_scalar_prefetch=1,
            grid=(n,),
            in_specs=[pl.BlockSpec((rows, share), lambda s, t: (0, s * cores + t[half]))],
            out_specs=[pl.BlockSpec((1, rows, share), lambda s, t: (s, 0, 0)), pl.BlockSpec((8, 128), lambda s, t: (0, 0))],
        ),
        out_shape=[jax.ShapeDtypeStruct((n, rows, share), BF16), jax.ShapeDtypeStruct((8, 128), F32)],
        compiler_params=params(MATMUL_MIB),
        cost_estimate=pl.CostEstimate(flops=0, bytes_accessed=4 * n * rows * share, transcendentals=0),
        name="expand_blocks",
    )(scalars, expand.reshape(rows, width))


def tie_kernel(*refs):
    pass


def tie(array, after):
    return pl.pallas_call(
        tie_kernel,
        in_specs=[pl.BlockSpec(memory_space=pl.ANY)] * (1 + len(after)),
        out_specs=pl.BlockSpec(memory_space=pl.ANY),
        out_shape=jax.ShapeDtypeStruct(array.shape, array.dtype),
        input_output_aliases={0: 0},
        compiler_params=params(1),
        name="tie",
    )(array, *after)


def matmul_kernel(n, waits, spans, half, sides, narrow, has_acc, token, scalars, *refs):
    refs = list(refs)[waits:]
    pieces = [[refs.pop(0) for _ in range(n)] for _ in spans]
    down = refs.pop(0)
    shrink = refs.pop(0)
    outs = len(sides) + narrow
    before = [refs.pop(0) for _ in range(outs)] if has_acc else []
    acc = [refs.pop(0) for _ in range(outs)]
    if token:
        refs.pop(0)[...] = jnp.zeros((8, 128), F32)
    tiles = [(part, at, tile) for part, (_, _, cuts) in enumerate(spans) for at, tile in cuts]
    lefts = [refs.pop(0) for _ in tiles]
    weights = [[refs.pop(0) for _ in tiles] for _ in sides]
    ranks = [refs.pop(0) for _ in tiles] if narrow else []
    earlier = [refs.pop(0) for _ in before]
    sems, old_sems = refs
    rows = pieces[0][0].shape[0]
    share = down.shape[1] // 2

    copies = []
    for k, (part, at, tile) in enumerate(tiles):
        base, start, _ = spans[part]
        group = []
        for i in range(n):
            to = pl.multiple_of(scalars[base + i] * rows, rows)
            group.append((pieces[part][i].at[:, pl.ds(at, tile)], lefts[k].at[pl.ds(to, rows), :]))
        if narrow:
            group.append((shrink.at[:, pl.ds(start + at, tile)], ranks[k]))
        for i, side in enumerate(sides):
            column = pl.multiple_of(scalars[half + side] * share, share)
            group.append((down.at[pl.ds(start + at, tile), pl.ds(column, share)], weights[i][k]))
        copies.append([pltpu.make_async_copy(*pair, sems.at[k, i]) for i, pair in enumerate(group)])
        for copy in copies[-1]:
            copy.start()
    old = [pltpu.make_async_copy(a, b, old_sems.at[i]) for i, (a, b) in enumerate(zip(before, earlier))]
    for copy in old:
        copy.start()

    for k in range(len(tiles)):
        for copy in copies[k]:
            copy.wait()
        left = lefts[k][...]
        terms = [jnp.dot(left, weights[i][k][...], preferred_element_type=F32) for i in range(len(sides))]
        if narrow:
            terms.append(
                lax.dot_general(ranks[k][...], left, (((1,), (1,)), ((), ())), preferred_element_type=F32)
            )
        for i, term in enumerate(terms):
            acc[i][...] = term if k == 0 else acc[i][...] + term
    for i, copy in enumerate(old):
        copy.wait()
        acc[i][...] += earlier[i][...]


def cuts_of(width, most):
    count = -(-width // most)
    sizes = [width - most * (count - 1)] + [most] * (count - 1)
    return [(sum(sizes[:i]), size) for i, size in enumerate(sizes)]


def chunk_matmul(scalars, half, chunks, down, shrink, acc, sides, narrow, label, after=(), token=False):
    n = len(chunks[0][0])
    rows = chunks[0][0][0].shape[0] * n
    share = down.shape[1] // 2
    ranks = shrink.shape[0]
    spans = [(base, start, cuts_of(pieces[0].shape[1], TILE if sides else 2 * TILE)) for pieces, base, start in chunks]
    sizes = [tile for _, _, cuts in spans for _, tile in cuts]
    width = sum(sizes)
    anywhere = pl.BlockSpec(memory_space=pl.ANY)
    args = [*after, *(piece for pieces, _, _ in chunks for piece in pieces), down, shrink, *(acc or ())]
    shapes = [(rows, share)] * len(sides) + [(ranks, rows)] * narrow
    marks = [(8, 128)] * token
    columns = share * len(sides) + ranks * narrow
    return pl.pallas_call(
        functools.partial(matmul_kernel, n, len(after), spans, half, sides, narrow, acc is not None, token),
        grid_spec=pltpu.PrefetchScalarGridSpec(
            num_scalar_prefetch=1,
            grid=(),
            in_specs=[anywhere] * len(args),
            out_specs=[pl.BlockSpec(memory_space=pltpu.VMEM)] * len(shapes + marks),
            scratch_shapes=[pltpu.VMEM((rows, tile), BF16) for tile in sizes]
            + [pltpu.VMEM((tile, share), BF16) for _ in sides for tile in sizes]
            + [pltpu.VMEM((ranks, tile), BF16) for tile in sizes if narrow]
            + [pltpu.VMEM(shape, F32) for shape in shapes if acc is not None]
            + [pltpu.SemaphoreType.DMA((len(sizes), n + 3)), pltpu.SemaphoreType.DMA((3,))],
        ),
        out_shape=[jax.ShapeDtypeStruct(shape, F32) for shape in shapes + marks],
        compiler_params=params(MATMUL_MIB),
        cost_estimate=pl.CostEstimate(
            flops=4 * rows * width * columns,
            bytes_accessed=2 * width * (columns + rows) + 8 * rows * columns,
            transcendentals=0,
        ),
        name=label,
    )(scalars, *args)


def final_kernel(n, owned, shrunk, slot, factors, kept, other, out, spread):
    rank = shrunk.shape[0]
    wide = owned * rank
    rows = out.shape[0]
    lane = lax.broadcasted_iota(jnp.int32, (rows, wide), 1) // rank
    own = shrunk[...].astype(F32).T
    pair = jnp.concatenate([own] * owned, axis=1)
    place = slot[...] - lane
    for i in range(n):
        spread[:, i * wide:(i + 1) * wide] = jnp.where(place == i * owned, pair, 0.0).astype(BF16)
    extra = jnp.dot(spread[...], factors[...], preferred_element_type=F32)
    out[...] = (kept[...] + other[...] + extra).astype(BF16)


def final(shrunk, slot_column, factors, kept, other, owned):
    n, wide, share = factors.shape
    rows = kept.shape[0]
    return pl.pallas_call(
        functools.partial(final_kernel, n, owned),
        in_specs=[pl.BlockSpec(memory_space=pltpu.VMEM)] * 5,
        out_specs=pl.BlockSpec(memory_space=pltpu.VMEM),
        scratch_shapes=[pltpu.VMEM((rows, n * wide), BF16)],
        out_shape=jax.ShapeDtypeStruct((rows, share), BF16),
        compiler_params=params(MATMUL_MIB),
        cost_estimate=pl.CostEstimate(
            flops=2 * rows * share * n * wide,
            bytes_accessed=2 * n * wide * share + 10 * rows * share,
            transcendentals=0,
        ),
        name="expand_and_add",
    )(shrunk, slot_column, factors.reshape(n * wide, share), kept, other)


def make_shards(n, cores):
    order = ring_order(n)
    place_of = {store: place for place, store in enumerate(order)}
    clockwise = [(order[i], order[(i + 1) % n]) for i in range(n)]
    counter = [(order[i], order[i - 1]) for i in range(n)]
    long, short = n // 2, (n - 1) // 2
    swap = [(t, (t + 1) % cores) for t in range(cores)]
    hops = [[0] + [-i for i in range(1, a + 1)] + list(range(1, b + 1)) for a, b in ((long, short), (short, long))]
    table = np.array(
        [
            [order[(place_of[s] + hop) % n] for way in hops for hop in way] + [t, 1 - t]
            for s in range(n)
            for t in range(cores)
        ],
        np.int32,
    )
    half = 2 * n

    def shards(hidden, down, shrink, expand, row_adapter, adapter_slot):
        owned, units, rank = shrink.shape
        store, tensor = lax.axis_index("store"), lax.axis_index("tensor")
        scalars = lax.dynamic_slice_in_dim(jnp.asarray(table), store * cores + tensor, 1, 0)[0]
        shrink_rows = jnp.transpose(shrink, (0, 2, 1)).reshape(owned * rank, units)

        slots = jnp.arange(adapter_slot.shape[0], dtype=jnp.int32)
        row_slot = jnp.sum(jnp.where(row_adapter[None, :] == slots[:, None], adapter_slot[:, None], 0), axis=0)

        small = 3 * units // 14
        widths = [small, units // 2 - small, units // 2 - small, small]
        starts = [sum(widths[:chunk]) for chunk in range(4)]

        def ring(chunk, own, held=None):
            way = chunk % 2
            pieces = [own]
            for turn, length in enumerate(((long, short), (short, long))[way]):
                moving = own
                for step in range(1, length + 1):
                    moving = lax.ppermute(moving, "store", (clockwise, counter)[turn])
                    if held and turn == 0 and step == held[0]:
                        moving = tie(moving, held[1:])
                    pieces.append(moving)
            ends = [pieces[((long, short), (short, long))[way][0]], pieces[-1]]
            return (pieces, way * n, starts[chunk]), ends

        call = functools.partial(chunk_matmul, scalars, half)
        own = [hidden[:, at:at + width] for at, width in zip(starts, widths)]
        blocks, mark = expand_blocks(scalars, half, expand, n, cores)
        chunk_0, ends_0 = ring(0, own[0], (2, mark))
        chunk_1, ends_1 = ring(1, own[1])
        *acc, token = call([chunk_0], down, shrink_rows, None, (0, 1), True, "chunk_0", token=True)
        chunk_2, ends_2 = ring(2, tie(own[2], ends_0), (1, token))
        *acc, token = call([chunk_1], down, shrink_rows, acc, (0, 1), True, "chunk_1", token=True)
        chunk_3, ends_3 = ring(3, tie(own[3], ends_1), (1, token))
        factors = lax.all_to_all(tie(blocks, ends_2), "store", 0, 0)
        last = [chunk_2, chunk_3]
        narrow, = call(last, down, shrink_rows, acc[2:], (), True, "last_narrow")
        mine = [
            jnp.where((row_slot == store * owned + i)[None, :], narrow[i * rank:(i + 1) * rank], 0.0)
            for i in range(owned)
        ]
        mine = sum(mine[1:], mine[0])
        send, = call(last, down, shrink_rows, acc[1:2], (1,), False, "last_sent", [mine])
        kept, = call(last, down, shrink_rows, acc[:1], (0,), False, "last_kept", [send])
        where = [(s, t) for s in range(n) for t in range(cores)]
        whole = mine
        for ds in range(2):
            for dt in range(cores):
                if ds or dt:
                    pairs = [(s * cores + t, (s ^ ds) * cores + (t + dt) % cores) for s, t in where]
                    whole = whole + lax.ppermute(mine, ("store", "tensor"), pairs)
        column = whole.astype(BF16)
        shrunk = column
        for ds in range(2, n, 2):
            shrunk = shrunk + lax.ppermute(column, "store", [(s, (s + ds) % n) for s in range(n)])
        other = lax.ppermute(send, "tensor", swap)
        return final(shrunk, row_slot[:, None], factors, kept, other, owned)

    return shards


def solution(mesh):
    in_specs = (
        P(("parts", "store"), "tensor"),
        P("tensor", "store"),
        P(("parts", "store"), "tensor", None),
        P(("parts", "store"), None, None),
        P("parts"),
        P("parts"),
    )
    out_specs = P("parts", ("store", "tensor"))
    shards = make_shards(mesh.shape["store"], mesh.shape["tensor"])
    return jax.shard_map(shards, mesh=mesh, in_specs=in_specs, out_specs=out_specs, check_vma=False)
```

```python
import functools

import jax
import jax.numpy as jnp
import numpy as np
from jax import lax
from jax.experimental import pallas as pl
from jax.experimental.pallas import tpu as pltpu
from jax.sharding import PartitionSpec as P

F32, BF16 = jnp.float32, jnp.bfloat16
TILE = 1024
CHUNKS = 4
MIB = 2**20
MATMUL_MIB = 28


def params(mib):
    return pltpu.CompilerParams(vmem_limit_bytes=mib * MIB)


def ring_order(n):
    return list(range(0, n, 2)) + list(range(1, n, 2))[::-1]


def split_kernel(scalars, src, dst, mark):
    dst[...] = src[...][None]
    mark[...] = jnp.zeros_like(mark)


def expand_blocks(scalars, half, expand, n, cores):
    owned, rank, width = expand.shape
    rows = owned * rank
    share = width // (n * cores)
    return pl.pallas_call(
        split_kernel,
        grid_spec=pltpu.PrefetchScalarGridSpec(
            num_scalar_prefetch=1,
            grid=(n,),
            in_specs=[pl.BlockSpec((rows, share), lambda s, t: (0, s * cores + t[half]))],
            out_specs=[pl.BlockSpec((1, rows, share), lambda s, t: (s, 0, 0)), pl.BlockSpec((8, 128), lambda s, t: (0, 0))],
        ),
        out_shape=[jax.ShapeDtypeStruct((n, rows, share), BF16), jax.ShapeDtypeStruct((8, 128), F32)],
        compiler_params=params(4),
        cost_estimate=pl.CostEstimate(flops=0, bytes_accessed=4 * n * rows * share, transcendentals=0),
        name="expand_blocks",
    )(scalars, expand.reshape(rows, width))


def tie_kernel(*refs):
    pass


def tie(array, after):
    return pl.pallas_call(
        tie_kernel,
        in_specs=[pl.BlockSpec(memory_space=pl.ANY)] * (1 + len(after)),
        out_specs=pl.BlockSpec(memory_space=pl.ANY),
        out_shape=jax.ShapeDtypeStruct(array.shape, array.dtype),
        input_output_aliases={0: 0},
        compiler_params=params(1),
        name="tie",
    )(array, *after)


def matmul_kernel(n, waits, spans, half, sides, narrow, has_acc, scalars, *refs):
    refs = list(refs)[waits:]
    pieces = [[refs.pop(0) for _ in range(n)] for _ in spans]
    down = refs.pop(0)
    shrink = refs.pop(0)
    outs = len(sides) + narrow
    before = [refs.pop(0) for _ in range(outs)] if has_acc else []
    acc = [refs.pop(0) for _ in range(outs)]
    tiles = [(part, at, tile) for part, (_, _, cuts) in enumerate(spans) for at, tile in cuts]
    lefts = [refs.pop(0) for _ in tiles]
    weights = [[refs.pop(0) for _ in tiles] for _ in sides]
    ranks = [refs.pop(0) for _ in tiles] if narrow else []
    earlier = [refs.pop(0) for _ in before]
    sems, old_sems = refs
    rows = pieces[0][0].shape[0]
    share = down.shape[1] // 2

    copies = []
    for k, (part, at, tile) in enumerate(tiles):
        base, start, _ = spans[part]
        group = []
        for i in range(n):
            to = pl.multiple_of(scalars[base + i] * rows, rows)
            group.append((pieces[part][i].at[:, pl.ds(at, tile)], lefts[k].at[pl.ds(to, rows), :]))
        if narrow:
            group.append((shrink.at[:, pl.ds(start + at, tile)], ranks[k]))
        for i, side in enumerate(sides):
            column = pl.multiple_of(scalars[half + side] * share, share)
            group.append((down.at[pl.ds(start + at, tile), pl.ds(column, share)], weights[i][k]))
        copies.append([pltpu.make_async_copy(*pair, sems.at[k, i]) for i, pair in enumerate(group)])
        for copy in copies[-1]:
            copy.start()
    old = [pltpu.make_async_copy(a, b, old_sems.at[i]) for i, (a, b) in enumerate(zip(before, earlier))]
    for copy in old:
        copy.start()

    for k in range(len(tiles)):
        for copy in copies[k]:
            copy.wait()
        left = lefts[k][...]
        terms = [jnp.dot(left, weights[i][k][...], preferred_element_type=F32) for i in range(len(sides))]
        if narrow:
            terms.append(
                lax.dot_general(ranks[k][...], left, (((1,), (1,)), ((), ())), preferred_element_type=F32)
            )
        for i, term in enumerate(terms):
            acc[i][...] = term if k == 0 else acc[i][...] + term
    for i, copy in enumerate(old):
        copy.wait()
        acc[i][...] += earlier[i][...]


def cuts_of(width):
    first = width % TILE or TILE
    sizes = [first // 2] * 2 if first == TILE else [first]
    sizes += [TILE] * ((width - first) // TILE)
    return [(sum(sizes[:i]), size) for i, size in enumerate(sizes)]


def chunk_matmul(scalars, half, chunks, down, shrink, acc, sides, narrow, label, after=()):
    n = len(chunks[0][0])
    rows = chunks[0][0][0].shape[0] * n
    share = down.shape[1] // 2
    ranks = shrink.shape[0]
    spans = [(base, start, cuts_of(pieces[0].shape[1])) for pieces, base, start in chunks]
    sizes = [tile for _, _, cuts in spans for _, tile in cuts]
    width = sum(sizes)
    anywhere = pl.BlockSpec(memory_space=pl.ANY)
    args = [*after, *(piece for pieces, _, _ in chunks for piece in pieces), down, shrink, *(acc or ())]
    shapes = [(rows, share)] * len(sides) + [(ranks, rows)] * narrow
    columns = share * len(sides) + ranks * narrow
    return pl.pallas_call(
        functools.partial(matmul_kernel, n, len(after), spans, half, sides, narrow, acc is not None),
        grid_spec=pltpu.PrefetchScalarGridSpec(
            num_scalar_prefetch=1,
            grid=(),
            in_specs=[anywhere] * len(args),
            out_specs=[pl.BlockSpec(memory_space=pltpu.VMEM)] * len(shapes),
            scratch_shapes=[pltpu.VMEM((rows, tile), BF16) for tile in sizes]
            + [pltpu.VMEM((tile, share), BF16) for _ in sides for tile in sizes]
            + [pltpu.VMEM((ranks, tile), BF16) for tile in sizes if narrow]
            + [pltpu.VMEM(shape, F32) for shape in shapes if acc is not None]
            + [pltpu.SemaphoreType.DMA((len(sizes), n + 3)), pltpu.SemaphoreType.DMA((3,))],
        ),
        out_shape=[jax.ShapeDtypeStruct(shape, F32) for shape in shapes],
        compiler_params=params(MATMUL_MIB),
        cost_estimate=pl.CostEstimate(
            flops=4 * rows * width * columns,
            bytes_accessed=2 * width * (columns + rows) + 8 * rows * columns,
            transcendentals=0,
        ),
        name=label,
    )(scalars, *args)


def final_kernel(n, owned, shrunk, slot, factors, kept, other, out, spread):
    rank = shrunk.shape[0]
    wide = owned * rank
    rows = out.shape[0]
    lane = lax.broadcasted_iota(jnp.int32, (rows, wide), 1) // rank
    own = shrunk[...].astype(F32).T
    pair = jnp.concatenate([own] * owned, axis=1)
    place = slot[...] - lane
    for i in range(n):
        spread[:, i * wide:(i + 1) * wide] = jnp.where(place == i * owned, pair, 0.0).astype(BF16)
    extra = jnp.dot(spread[...], factors[...], preferred_element_type=F32)
    out[...] = (kept[...] + other[...] + extra).astype(BF16)


def final(shrunk, slot_column, factors, kept, other, owned):
    n, wide, share = factors.shape
    rows = kept.shape[0]
    return pl.pallas_call(
        functools.partial(final_kernel, n, owned),
        in_specs=[pl.BlockSpec(memory_space=pltpu.VMEM)] * 5,
        out_specs=pl.BlockSpec(memory_space=pltpu.VMEM),
        scratch_shapes=[pltpu.VMEM((rows, n * wide), BF16)],
        out_shape=jax.ShapeDtypeStruct((rows, share), BF16),
        compiler_params=params(8),
        cost_estimate=pl.CostEstimate(
            flops=2 * rows * share * n * wide,
            bytes_accessed=2 * n * wide * share + 10 * rows * share,
            transcendentals=0,
        ),
        name="expand_and_add",
    )(shrunk, slot_column, factors.reshape(n * wide, share), kept, other)


def make_shards(n, cores):
    order = ring_order(n)
    place_of = {store: place for place, store in enumerate(order)}
    clockwise = [(order[i], order[(i + 1) % n]) for i in range(n)]
    counter = [(order[i], order[i - 1]) for i in range(n)]
    long, short = n // 2, (n - 1) // 2
    swap = [(t, (t + 1) % cores) for t in range(cores)]
    hops = [[0] + [-i for i in range(1, a + 1)] + list(range(1, b + 1)) for a, b in ((long, short), (short, long))]
    table = np.array(
        [
            [order[(place_of[s] + hop) % n] for way in hops for hop in way] + [t, 1 - t]
            for s in range(n)
            for t in range(cores)
        ],
        np.int32,
    )
    half = 2 * n

    def shards(hidden, down, shrink, expand, row_adapter, adapter_slot):
        owned, units, rank = shrink.shape
        store, tensor = lax.axis_index("store"), lax.axis_index("tensor")
        scalars = lax.dynamic_slice_in_dim(jnp.asarray(table), store * cores + tensor, 1, 0)[0]
        shrink_rows = jnp.transpose(shrink, (0, 2, 1)).reshape(owned * rank, units)

        slots = jnp.arange(adapter_slot.shape[0], dtype=jnp.int32)
        row_slot = jnp.sum(jnp.where(row_adapter[None, :] == slots[:, None], adapter_slot[:, None], 0), axis=0)

        width = units // CHUNKS
        blocks, mark = expand_blocks(scalars, half, expand, n, cores)
        chunks, ends = [], []
        for chunk in range(CHUNKS):
            start = chunk * width
            own = hidden[:, start:start + width]
            if chunk == CHUNKS - 1:
                own = tie(own, [mark])
            way = chunk % 2
            pieces = [own]
            for length, pairs in zip(((long, short), (short, long))[way], (clockwise, counter)):
                moving = own
                for step in range(length):
                    moving = lax.ppermute(moving, "store", pairs)
                    pieces.append(moving)
                ends.append(moving)
            chunks.append((pieces, way * n, start))
        factors = lax.all_to_all(tie(blocks, ends[:4]), "store", 0, 0)

        call = functools.partial(chunk_matmul, scalars, half)
        first, last = chunks[:CHUNKS // 2], chunks[CHUNKS // 2:]
        acc = call(first, down, shrink_rows, None, (0, 1), True, "first_chunks")
        narrow, = call(last, down, shrink_rows, acc[2:], (), True, "last_narrow")
        mine = [
            jnp.where((row_slot == store * owned + i)[None, :], narrow[i * rank:(i + 1) * rank], 0.0)
            for i in range(owned)
        ]
        mine = sum(mine[1:], mine[0])
        send, = call(last, down, shrink_rows, acc[1:2], (1,), False, "last_sent", [mine])
        kept, = call(last, down, shrink_rows, acc[:1], (0,), False, "last_kept", [send])
        where = [(s, t) for s in range(n) for t in range(cores)]
        whole = mine
        for ds in range(2):
            for dt in range(cores):
                if ds or dt:
                    pairs = [(s * cores + t, (s ^ ds) * cores + (t + dt) % cores) for s, t in where]
                    whole = whole + lax.ppermute(mine, ("store", "tensor"), pairs)
        column = whole.astype(BF16)
        shrunk = column
        for ds in range(2, n, 2):
            shrunk = shrunk + lax.ppermute(column, "store", [(s, (s + ds) % n) for s in range(n)])
        other = lax.ppermute(send, "tensor", swap)
        return final(shrunk, row_slot[:, None], factors, kept, other, owned)

    return shards


def solution(mesh):
    in_specs = (
        P(("parts", "store"), "tensor"),
        P("tensor", "store"),
        P(("parts", "store"), "tensor", None),
        P(("parts", "store"), None, None),
        P("parts"),
        P("parts"),
    )
    out_specs = P("parts", ("store", "tensor"))
    shards = make_shards(mesh.shape["store"], mesh.shape["tensor"])
    return jax.shard_map(shards, mesh=mesh, in_specs=in_specs, out_specs=out_specs, check_vma=False)
```

```python
import functools

import jax
import jax.numpy as jnp
import numpy as np
from jax import lax
from jax.experimental import pallas as pl
from jax.experimental.pallas import tpu as pltpu
from jax.sharding import PartitionSpec as P

F32, BF16 = jnp.float32, jnp.bfloat16
TILE = 1024
CHUNKS = 4
MIB = 2**20
MATMUL_MIB = 28


def params(mib):
    return pltpu.CompilerParams(vmem_limit_bytes=mib * MIB)


placed = pltpu.with_memory_space_constraint


def ring_order(n):
    return list(range(0, n, 2)) + list(range(1, n, 2))[::-1]


def split_kernel(scalars, src, dst, mark):
    dst[...] = src[...][None]
    mark[...] = jnp.zeros_like(mark)


def expand_blocks(scalars, half, expand, n, cores):
    owned, rank, width = expand.shape
    rows = owned * rank
    share = width // (n * cores)
    return pl.pallas_call(
        split_kernel,
        grid_spec=pltpu.PrefetchScalarGridSpec(
            num_scalar_prefetch=1,
            grid=(n,),
            in_specs=[pl.BlockSpec((rows, share), lambda s, t: (0, s * cores + t[half]))],
            out_specs=[pl.BlockSpec((1, rows, share), lambda s, t: (s, 0, 0)), pl.BlockSpec((8, 128), lambda s, t: (0, 0))],
        ),
        out_shape=[jax.ShapeDtypeStruct((n, rows, share), BF16), jax.ShapeDtypeStruct((8, 128), F32)],
        compiler_params=params(4),
        cost_estimate=pl.CostEstimate(flops=0, bytes_accessed=4 * n * rows * share, transcendentals=0),
        name="expand_blocks",
    )(scalars, expand.reshape(rows, width))


def tie_kernel(*refs):
    pass


def tie(array, after):
    return pl.pallas_call(
        tie_kernel,
        in_specs=[pl.BlockSpec(memory_space=pl.ANY)] * (1 + len(after)),
        out_specs=pl.BlockSpec(memory_space=pl.ANY),
        out_shape=jax.ShapeDtypeStruct(array.shape, array.dtype),
        input_output_aliases={0: 0},
        compiler_params=params(1),
        name="tie",
    )(array, *after)


def matmul_kernel(n, waits, spans, half, sides, narrow, has_acc, scalars, *refs):
    refs = list(refs)[waits:]
    pieces = [[refs.pop(0) for _ in range(n)] for _ in spans]
    down = refs.pop(0)
    shrink = refs.pop(0)
    outs = len(sides) + narrow
    before = [refs.pop(0) for _ in range(outs)] if has_acc else []
    acc = [refs.pop(0) for _ in range(outs)]
    tiles = [(part, at, tile) for part, (_, _, cuts) in enumerate(spans) for at, tile in cuts]
    lefts = [refs.pop(0) for _ in tiles]
    weights = [[refs.pop(0) for _ in tiles] for _ in sides]
    ranks = [refs.pop(0) for _ in tiles] if narrow else []
    earlier = [refs.pop(0) for _ in before]
    sems, old_sems = refs
    rows = pieces[0][0].shape[0]
    share = down.shape[1] // 2

    copies = []
    for k, (part, at, tile) in enumerate(tiles):
        base, start, _ = spans[part]
        group = []
        for i in range(n):
            to = pl.multiple_of(scalars[base + i] * rows, rows)
            group.append((pieces[part][i].at[:, pl.ds(at, tile)], lefts[k].at[pl.ds(to, rows), :]))
        if narrow:
            group.append((shrink.at[:, pl.ds(start + at, tile)], ranks[k]))
        for i, side in enumerate(sides):
            column = pl.multiple_of(scalars[half + side] * share, share)
            group.append((down.at[pl.ds(start + at, tile), pl.ds(column, share)], weights[i][k]))
        copies.append([pltpu.make_async_copy(*pair, sems.at[k, i]) for i, pair in enumerate(group)])
        for copy in copies[-1]:
            copy.start()
    old = [pltpu.make_async_copy(a, b, old_sems.at[i]) for i, (a, b) in enumerate(zip(before, earlier))]
    for copy in old:
        copy.start()

    for k in range(len(tiles)):
        for copy in copies[k]:
            copy.wait()
        left = lefts[k][...]
        terms = [jnp.dot(left, weights[i][k][...], preferred_element_type=F32) for i in range(len(sides))]
        if narrow:
            terms.append(
                lax.dot_general(ranks[k][...], left, (((1,), (1,)), ((), ())), preferred_element_type=F32)
            )
        for i, term in enumerate(terms):
            acc[i][...] = term if k == 0 else acc[i][...] + term
    for i, copy in enumerate(old):
        copy.wait()
        acc[i][...] += earlier[i][...]


def cuts_of(width):
    first = width % TILE or TILE
    sizes = [first // 2] * 2 if first == TILE else [first]
    sizes += [TILE] * ((width - first) // TILE)
    return [(sum(sizes[:i]), size) for i, size in enumerate(sizes)]


def chunk_matmul(scalars, half, chunks, down, shrink, acc, sides, narrow, label, after=()):
    n = len(chunks[0][0])
    rows = chunks[0][0][0].shape[0] * n
    share = down.shape[1] // 2
    ranks = shrink.shape[0]
    spans = [(base, start, cuts_of(pieces[0].shape[1])) for pieces, base, start in chunks]
    sizes = [tile for _, _, cuts in spans for _, tile in cuts]
    width = sum(sizes)
    anywhere = pl.BlockSpec(memory_space=pl.ANY)
    held = [placed(piece, pltpu.VMEM) for pieces, _, _ in chunks for piece in pieces]
    args = [*after, *held, placed(down, pltpu.HBM), placed(shrink, pltpu.HBM), *(acc or ())]
    shapes = [(rows, share)] * len(sides) + [(ranks, rows)] * narrow
    columns = share * len(sides) + ranks * narrow
    return pl.pallas_call(
        functools.partial(matmul_kernel, n, len(after), spans, half, sides, narrow, acc is not None),
        grid_spec=pltpu.PrefetchScalarGridSpec(
            num_scalar_prefetch=1,
            grid=(),
            in_specs=[anywhere] * len(args),
            out_specs=[pl.BlockSpec(memory_space=pltpu.VMEM)] * len(shapes),
            scratch_shapes=[pltpu.VMEM((rows, tile), BF16) for tile in sizes]
            + [pltpu.VMEM((tile, share), BF16) for _ in sides for tile in sizes]
            + [pltpu.VMEM((ranks, tile), BF16) for tile in sizes if narrow]
            + [pltpu.VMEM(shape, F32) for shape in shapes if acc is not None]
            + [pltpu.SemaphoreType.DMA((len(sizes), n + 3)), pltpu.SemaphoreType.DMA((3,))],
        ),
        out_shape=[jax.ShapeDtypeStruct(shape, F32) for shape in shapes],
        compiler_params=params(MATMUL_MIB),
        cost_estimate=pl.CostEstimate(
            flops=4 * rows * width * columns,
            bytes_accessed=2 * width * (columns + rows) + 8 * rows * columns,
            transcendentals=0,
        ),
        name=label,
    )(scalars, *args)


def final_kernel(n, owned, shrunk, slot, factors, kept, other, out, spread):
    rank = shrunk.shape[0]
    wide = owned * rank
    rows = out.shape[0]
    lane = lax.broadcasted_iota(jnp.int32, (rows, wide), 1) // rank
    own = shrunk[...].astype(F32).T
    pair = jnp.concatenate([own] * owned, axis=1)
    place = slot[...] - lane
    for i in range(n):
        spread[:, i * wide:(i + 1) * wide] = jnp.where(place == i * owned, pair, 0.0).astype(BF16)
    extra = jnp.dot(spread[...], factors[...], preferred_element_type=F32)
    out[...] = (kept[...] + other[...] + extra).astype(BF16)


def final(shrunk, slot_column, factors, kept, other, owned):
    n, wide, share = factors.shape
    rows = kept.shape[0]
    return pl.pallas_call(
        functools.partial(final_kernel, n, owned),
        in_specs=[pl.BlockSpec(memory_space=pltpu.VMEM)] * 5,
        out_specs=pl.BlockSpec(memory_space=pltpu.VMEM),
        scratch_shapes=[pltpu.VMEM((rows, n * wide), BF16)],
        out_shape=jax.ShapeDtypeStruct((rows, share), BF16),
        compiler_params=params(8),
        cost_estimate=pl.CostEstimate(
            flops=2 * rows * share * n * wide,
            bytes_accessed=2 * n * wide * share + 10 * rows * share,
            transcendentals=0,
        ),
        name="expand_and_add",
    )(shrunk, slot_column, factors.reshape(n * wide, share), kept, other)


def make_shards(n, cores):
    order = ring_order(n)
    place_of = {store: place for place, store in enumerate(order)}
    clockwise = [(order[i], order[(i + 1) % n]) for i in range(n)]
    counter = [(order[i], order[i - 1]) for i in range(n)]
    long, short = n // 2, (n - 1) // 2
    swap = [(t, (t + 1) % cores) for t in range(cores)]
    hops = [[0] + [-i for i in range(1, a + 1)] + list(range(1, b + 1)) for a, b in ((long, short), (short, long))]
    table = np.array(
        [
            [order[(place_of[s] + hop) % n] for way in hops for hop in way] + [t, 1 - t]
            for s in range(n)
            for t in range(cores)
        ],
        np.int32,
    )
    half = 2 * n

    def shards(hidden, down, shrink, expand, row_adapter, adapter_slot):
        owned, units, rank = shrink.shape
        store, tensor = lax.axis_index("store"), lax.axis_index("tensor")
        scalars = lax.dynamic_slice_in_dim(jnp.asarray(table), store * cores + tensor, 1, 0)[0]
        shrink_rows = jnp.transpose(shrink, (0, 2, 1)).reshape(owned * rank, units)

        slots = jnp.arange(adapter_slot.shape[0], dtype=jnp.int32)
        row_slot = jnp.sum(jnp.where(row_adapter[None, :] == slots[:, None], adapter_slot[:, None], 0), axis=0)

        width = units // CHUNKS
        blocks, mark = expand_blocks(scalars, half, expand, n, cores)
        chunks, ends = [], []
        for chunk in range(CHUNKS):
            start = chunk * width
            own = hidden[:, start:start + width]
            if chunk == CHUNKS - 1:
                own = tie(own, [mark])
            way = chunk % 2
            pieces = [own]
            for length, pairs in zip(((long, short), (short, long))[way], (clockwise, counter)):
                moving = own
                for step in range(length):
                    moving = lax.ppermute(moving, "store", pairs)
                    pieces.append(moving)
                ends.append(moving)
            chunks.append((pieces, way * n, start))
        factors = lax.all_to_all(tie(blocks, ends[:4]), "store", 0, 0)

        call = functools.partial(chunk_matmul, scalars, half)
        first, last = chunks[:CHUNKS // 2], chunks[CHUNKS // 2:]
        acc = call(first, down, shrink_rows, None, (0, 1), True, "first_chunks")
        send, narrow = call(last, down, shrink_rows, acc[1:], (1,), True, "last_sent")
        mine = [
            jnp.where((row_slot == store * owned + i)[None, :], narrow[i * rank:(i + 1) * rank], 0.0)
            for i in range(owned)
        ]
        mine = sum(mine[1:], mine[0])
        kept, = call(last, down, shrink_rows, acc[:1], (0,), False, "last_kept", [mine])
        where = [(s, t) for s in range(n) for t in range(cores)]
        whole = mine
        for ds in range(2):
            for dt in range(cores):
                if ds or dt:
                    pairs = [(s * cores + t, (s ^ ds) * cores + (t + dt) % cores) for s, t in where]
                    whole = whole + lax.ppermute(mine, ("store", "tensor"), pairs)
        column = whole.astype(BF16)
        shrunk = column
        for ds in range(2, n, 2):
            shrunk = shrunk + lax.ppermute(column, "store", [(s, (s + ds) % n) for s in range(n)])
        other = lax.ppermute(send, "tensor", swap)
        return final(shrunk, row_slot[:, None], factors, kept, other, owned)

    return shards


def solution(mesh):
    in_specs = (
        P(("parts", "store"), "tensor"),
        P("tensor", "store"),
        P(("parts", "store"), "tensor", None),
        P(("parts", "store"), None, None),
        P("parts"),
        P("parts"),
    )
    out_specs = P("parts", ("store", "tensor"))
    shards = make_shards(mesh.shape["store"], mesh.shape["tensor"])
    return jax.shard_map(shards, mesh=mesh, in_specs=in_specs, out_specs=out_specs, check_vma=False)
```

```python
import functools

import jax
import jax.numpy as jnp
import numpy as np
from jax import lax
from jax.experimental import pallas as pl
from jax.experimental.pallas import tpu as pltpu
from jax.sharding import PartitionSpec as P

F32, BF16 = jnp.float32, jnp.bfloat16
TILE = 1024
CHUNKS = 4
MIB = 2**20
MATMUL_MIB = 28


def params(mib):
    return pltpu.CompilerParams(vmem_limit_bytes=mib * MIB)


def in_hbm(array):
    return pltpu.with_memory_space_constraint(array, pltpu.HBM)


def ring_order(n):
    return list(range(0, n, 2)) + list(range(1, n, 2))[::-1]


def split_kernel(scalars, src, dst, mark):
    dst[...] = src[...][None]
    mark[...] = jnp.zeros_like(mark)


def expand_blocks(scalars, half, expand, n, cores):
    owned, rank, width = expand.shape
    rows = owned * rank
    share = width // (n * cores)
    return pl.pallas_call(
        split_kernel,
        grid_spec=pltpu.PrefetchScalarGridSpec(
            num_scalar_prefetch=1,
            grid=(n,),
            in_specs=[pl.BlockSpec((rows, share), lambda s, t: (0, s * cores + t[half]))],
            out_specs=[pl.BlockSpec((1, rows, share), lambda s, t: (s, 0, 0)), pl.BlockSpec((8, 128), lambda s, t: (0, 0))],
        ),
        out_shape=[jax.ShapeDtypeStruct((n, rows, share), BF16), jax.ShapeDtypeStruct((8, 128), F32)],
        compiler_params=params(4),
        cost_estimate=pl.CostEstimate(flops=0, bytes_accessed=4 * n * rows * share, transcendentals=0),
        name="expand_blocks",
    )(scalars, expand.reshape(rows, width))


def tie_kernel(*refs):
    pass


def tie(array, after):
    return pl.pallas_call(
        tie_kernel,
        in_specs=[pl.BlockSpec(memory_space=pl.ANY)] * (1 + len(after)),
        out_specs=pl.BlockSpec(memory_space=pl.ANY),
        out_shape=jax.ShapeDtypeStruct(array.shape, array.dtype),
        input_output_aliases={0: 0},
        compiler_params=params(1),
        name="tie",
    )(array, *after)


def matmul_kernel(n, waits, spans, half, sides, narrow, has_acc, scalars, *refs):
    refs = list(refs)[waits:]
    pieces = [[refs.pop(0) for _ in range(n)] for _ in spans]
    down = refs.pop(0)
    shrink = refs.pop(0)
    outs = len(sides) + narrow
    before = [refs.pop(0) for _ in range(outs)] if has_acc else []
    acc = [refs.pop(0) for _ in range(outs)]
    tiles = [(part, at, tile) for part, (_, _, cuts) in enumerate(spans) for at, tile in cuts]
    lefts = [refs.pop(0) for _ in tiles]
    weights = [[refs.pop(0) for _ in tiles] for _ in sides]
    ranks = [refs.pop(0) for _ in tiles] if narrow else []
    earlier = [refs.pop(0) for _ in before]
    sems, old_sems = refs
    rows = pieces[0][0].shape[0]
    share = down.shape[1] // 2

    copies = []
    for k, (part, at, tile) in enumerate(tiles):
        base, start, _ = spans[part]
        group = []
        for i in range(n):
            to = pl.multiple_of(scalars[base + i] * rows, rows)
            group.append((pieces[part][i].at[:, pl.ds(at, tile)], lefts[k].at[pl.ds(to, rows), :]))
        if narrow:
            group.append((shrink.at[:, pl.ds(start + at, tile)], ranks[k]))
        for i, side in enumerate(sides):
            column = pl.multiple_of(scalars[half + side] * share, share)
            group.append((down.at[pl.ds(start + at, tile), pl.ds(column, share)], weights[i][k]))
        copies.append([pltpu.make_async_copy(*pair, sems.at[k, i]) for i, pair in enumerate(group)])
        for copy in copies[-1]:
            copy.start()
    old = [pltpu.make_async_copy(a, b, old_sems.at[i]) for i, (a, b) in enumerate(zip(before, earlier))]
    for copy in old:
        copy.start()

    for k in range(len(tiles)):
        for copy in copies[k]:
            copy.wait()
        left = lefts[k][...]
        terms = [jnp.dot(left, weights[i][k][...], preferred_element_type=F32) for i in range(len(sides))]
        if narrow:
            terms.append(
                lax.dot_general(ranks[k][...], left, (((1,), (1,)), ((), ())), preferred_element_type=F32)
            )
        for i, term in enumerate(terms):
            acc[i][...] = term if k == 0 else acc[i][...] + term
    for i, copy in enumerate(old):
        copy.wait()
        acc[i][...] += earlier[i][...]


def cuts_of(width):
    first = width % TILE or TILE
    sizes = [first // 2] * 2 if first == TILE else [first]
    sizes += [TILE] * ((width - first) // TILE)
    return [(sum(sizes[:i]), size) for i, size in enumerate(sizes)]


def chunk_matmul(scalars, half, chunks, down, shrink, acc, sides, narrow, label, after=()):
    n = len(chunks[0][0])
    rows = chunks[0][0][0].shape[0] * n
    share = down.shape[1] // 2
    ranks = shrink.shape[0]
    spans = [(base, start, cuts_of(pieces[0].shape[1])) for pieces, base, start in chunks]
    sizes = [tile for _, _, cuts in spans for _, tile in cuts]
    width = sum(sizes)
    anywhere = pl.BlockSpec(memory_space=pl.ANY)
    held = [
        piece if i in late else in_hbm(piece)
        for pieces, base, _ in chunks
        for late in [(3, 4, n - 1) if base == 0 else (3, n - 2, n - 1)]
        for i, piece in enumerate(pieces)
    ]
    args = [*after, *held, in_hbm(down), in_hbm(shrink), *(acc or ())]
    shapes = [(rows, share)] * len(sides) + [(ranks, rows)] * narrow
    columns = share * len(sides) + ranks * narrow
    return pl.pallas_call(
        functools.partial(matmul_kernel, n, len(after), spans, half, sides, narrow, acc is not None),
        grid_spec=pltpu.PrefetchScalarGridSpec(
            num_scalar_prefetch=1,
            grid=(),
            in_specs=[anywhere] * len(args),
            out_specs=[pl.BlockSpec(memory_space=pltpu.VMEM)] * len(shapes),
            scratch_shapes=[pltpu.VMEM((rows, tile), BF16) for tile in sizes]
            + [pltpu.VMEM((tile, share), BF16) for _ in sides for tile in sizes]
            + [pltpu.VMEM((ranks, tile), BF16) for tile in sizes if narrow]
            + [pltpu.VMEM(shape, F32) for shape in shapes if acc is not None]
            + [pltpu.SemaphoreType.DMA((len(sizes), n + 3)), pltpu.SemaphoreType.DMA((3,))],
        ),
        out_shape=[jax.ShapeDtypeStruct(shape, F32) for shape in shapes],
        compiler_params=params(MATMUL_MIB),
        cost_estimate=pl.CostEstimate(
            flops=4 * rows * width * columns,
            bytes_accessed=2 * width * (columns + rows) + 8 * rows * columns,
            transcendentals=0,
        ),
        name=label,
    )(scalars, *args)


def final_kernel(n, owned, shrunk, slot, factors, kept, other, out, spread):
    rank = shrunk.shape[0]
    wide = owned * rank
    rows = out.shape[0]
    lane = lax.broadcasted_iota(jnp.int32, (rows, wide), 1) // rank
    own = shrunk[...].astype(F32).T
    pair = jnp.concatenate([own] * owned, axis=1)
    place = slot[...] - lane
    for i in range(n):
        spread[:, i * wide:(i + 1) * wide] = jnp.where(place == i * owned, pair, 0.0).astype(BF16)
    extra = jnp.dot(spread[...], factors[...], preferred_element_type=F32)
    out[...] = (kept[...] + other[...] + extra).astype(BF16)


def final(shrunk, slot_column, factors, kept, other, owned):
    n, wide, share = factors.shape
    rows = kept.shape[0]
    return pl.pallas_call(
        functools.partial(final_kernel, n, owned),
        in_specs=[pl.BlockSpec(memory_space=pltpu.VMEM)] * 5,
        out_specs=pl.BlockSpec(memory_space=pltpu.VMEM),
        scratch_shapes=[pltpu.VMEM((rows, n * wide), BF16)],
        out_shape=jax.ShapeDtypeStruct((rows, share), BF16),
        compiler_params=params(8),
        cost_estimate=pl.CostEstimate(
            flops=2 * rows * share * n * wide,
            bytes_accessed=2 * n * wide * share + 10 * rows * share,
            transcendentals=0,
        ),
        name="expand_and_add",
    )(shrunk, slot_column, factors.reshape(n * wide, share), kept, other)


def make_shards(n, cores):
    order = ring_order(n)
    place_of = {store: place for place, store in enumerate(order)}
    clockwise = [(order[i], order[(i + 1) % n]) for i in range(n)]
    counter = [(order[i], order[i - 1]) for i in range(n)]
    long, short = n // 2, (n - 1) // 2
    swap = [(t, (t + 1) % cores) for t in range(cores)]
    hops = [[0] + [-i for i in range(1, a + 1)] + list(range(1, b + 1)) for a, b in ((long, short), (short, long))]
    table = np.array(
        [
            [order[(place_of[s] + hop) % n] for way in hops for hop in way] + [t, 1 - t]
            for s in range(n)
            for t in range(cores)
        ],
        np.int32,
    )
    half = 2 * n

    def shards(hidden, down, shrink, expand, row_adapter, adapter_slot):
        owned, units, rank = shrink.shape
        store, tensor = lax.axis_index("store"), lax.axis_index("tensor")
        scalars = lax.dynamic_slice_in_dim(jnp.asarray(table), store * cores + tensor, 1, 0)[0]
        shrink_rows = jnp.transpose(shrink, (0, 2, 1)).reshape(owned * rank, units)

        slots = jnp.arange(adapter_slot.shape[0], dtype=jnp.int32)
        row_slot = jnp.sum(jnp.where(row_adapter[None, :] == slots[:, None], adapter_slot[:, None], 0), axis=0)

        width = units // CHUNKS
        blocks, mark = expand_blocks(scalars, half, expand, n, cores)
        chunks, ends = [], []
        for chunk in range(CHUNKS):
            start = chunk * width
            own = hidden[:, start:start + width]
            if chunk == CHUNKS - 1:
                own = tie(own, [mark])
            way = chunk % 2
            pieces = [own]
            for length, pairs in zip(((long, short), (short, long))[way], (clockwise, counter)):
                moving = own
                for step in range(length):
                    moving = lax.ppermute(moving, "store", pairs)
                    pieces.append(moving)
                ends.append(moving)
            chunks.append((pieces, way * n, start))
        factors = lax.all_to_all(tie(blocks, ends[:4]), "store", 0, 0)

        call = functools.partial(chunk_matmul, scalars, half)
        first, last = chunks[:CHUNKS // 2], chunks[CHUNKS // 2:]
        acc = call(first, down, shrink_rows, None, (0, 1), True, "first_chunks")
        narrow, = call(last, down, shrink_rows, acc[2:], (), True, "last_narrow")
        mine = [
            jnp.where((row_slot == store * owned + i)[None, :], narrow[i * rank:(i + 1) * rank], 0.0)
            for i in range(owned)
        ]
        mine = sum(mine[1:], mine[0])
        send, = call(last, down, shrink_rows, acc[1:2], (1,), False, "last_sent", [mine])
        kept, = call(last, down, shrink_rows, acc[:1], (0,), False, "last_kept", [send])
        where = [(s, t) for s in range(n) for t in range(cores)]
        whole = mine
        for ds in range(2):
            for dt in range(cores):
                if ds or dt:
                    pairs = [(s * cores + t, (s ^ ds) * cores + (t + dt) % cores) for s, t in where]
                    whole = whole + lax.ppermute(mine, ("store", "tensor"), pairs)
        column = whole.astype(BF16)
        shrunk = column
        for ds in range(2, n, 2):
            shrunk = shrunk + lax.ppermute(column, "store", [(s, (s + ds) % n) for s in range(n)])
        other = lax.ppermute(send, "tensor", swap)
        return final(shrunk, row_slot[:, None], factors, kept, other, owned)

    return shards


def solution(mesh):
    in_specs = (
        P(("parts", "store"), "tensor"),
        P("tensor", "store"),
        P(("parts", "store"), "tensor", None),
        P(("parts", "store"), None, None),
        P("parts"),
        P("parts"),
    )
    out_specs = P("parts", ("store", "tensor"))
    shards = make_shards(mesh.shape["store"], mesh.shape["tensor"])
    return jax.shard_map(shards, mesh=mesh, in_specs=in_specs, out_specs=out_specs, check_vma=False)
```

```python
import functools

import jax
import jax.numpy as jnp
import numpy as np
from jax import lax
from jax.experimental import pallas as pl
from jax.experimental.pallas import tpu as pltpu
from jax.sharding import PartitionSpec as P

F32, BF16 = jnp.float32, jnp.bfloat16
TILE = 1024
CHUNKS = 4
MIB = 2**20
MATMUL_MIB = 28


def params(mib):
    return pltpu.CompilerParams(vmem_limit_bytes=mib * MIB)


def in_hbm(array):
    return pltpu.with_memory_space_constraint(array, pltpu.HBM)


def ring_order(n):
    return list(range(0, n, 2)) + list(range(1, n, 2))[::-1]


def split_kernel(scalars, src, dst, mark):
    dst[...] = src[...][None]
    mark[...] = jnp.zeros_like(mark)


def expand_blocks(scalars, half, expand, n, cores):
    owned, rank, width = expand.shape
    rows = owned * rank
    share = width // (n * cores)
    return pl.pallas_call(
        split_kernel,
        grid_spec=pltpu.PrefetchScalarGridSpec(
            num_scalar_prefetch=1,
            grid=(n,),
            in_specs=[pl.BlockSpec((rows, share), lambda s, t: (0, s * cores + t[half]))],
            out_specs=[pl.BlockSpec((1, rows, share), lambda s, t: (s, 0, 0)), pl.BlockSpec((8, 128), lambda s, t: (0, 0))],
        ),
        out_shape=[jax.ShapeDtypeStruct((n, rows, share), BF16), jax.ShapeDtypeStruct((8, 128), F32)],
        compiler_params=params(4),
        cost_estimate=pl.CostEstimate(flops=0, bytes_accessed=4 * n * rows * share, transcendentals=0),
        name="expand_blocks",
    )(scalars, expand.reshape(rows, width))


def tie_kernel(*refs):
    pass


def tie(array, after):
    return pl.pallas_call(
        tie_kernel,
        in_specs=[pl.BlockSpec(memory_space=pl.ANY)] * (1 + len(after)),
        out_specs=pl.BlockSpec(memory_space=pl.ANY),
        out_shape=jax.ShapeDtypeStruct(array.shape, array.dtype),
        input_output_aliases={0: 0},
        compiler_params=params(1),
        name="tie",
    )(array, *after)


def matmul_kernel(n, waits, spans, half, sides, narrow, has_acc, token, scalars, *refs):
    refs = list(refs)[waits:]
    pieces = [[refs.pop(0) for _ in range(n)] for _ in spans]
    down = refs.pop(0)
    shrink = refs.pop(0)
    outs = len(sides) + narrow
    before = [refs.pop(0) for _ in range(outs)] if has_acc else []
    acc = [refs.pop(0) for _ in range(outs)]
    if token:
        refs.pop(0)[...] = jnp.zeros((8, 128), F32)
    tiles = [(part, at, tile) for part, (_, _, cuts) in enumerate(spans) for at, tile in cuts]
    lefts = [refs.pop(0) for _ in tiles]
    weights = [[refs.pop(0) for _ in tiles] for _ in sides]
    ranks = [refs.pop(0) for _ in tiles] if narrow else []
    earlier = [refs.pop(0) for _ in before]
    sems, old_sems = refs
    rows = pieces[0][0].shape[0]
    share = down.shape[1] // 2

    copies = []
    for k, (part, at, tile) in enumerate(tiles):
        base, start, _ = spans[part]
        group = []
        for i in range(n):
            to = pl.multiple_of(scalars[base + i] * rows, rows)
            group.append((pieces[part][i].at[:, pl.ds(at, tile)], lefts[k].at[pl.ds(to, rows), :]))
        if narrow:
            group.append((shrink.at[:, pl.ds(start + at, tile)], ranks[k]))
        for i, side in enumerate(sides):
            column = pl.multiple_of(scalars[half + side] * share, share)
            group.append((down.at[pl.ds(start + at, tile), pl.ds(column, share)], weights[i][k]))
        copies.append([pltpu.make_async_copy(*pair, sems.at[k, i]) for i, pair in enumerate(group)])
        for copy in copies[-1]:
            copy.start()
    old = [pltpu.make_async_copy(a, b, old_sems.at[i]) for i, (a, b) in enumerate(zip(before, earlier))]
    for copy in old:
        copy.start()

    for k in range(len(tiles)):
        for copy in copies[k]:
            copy.wait()
        left = lefts[k][...]
        terms = [jnp.dot(left, weights[i][k][...], preferred_element_type=F32) for i in range(len(sides))]
        if narrow:
            terms.append(
                lax.dot_general(ranks[k][...], left, (((1,), (1,)), ((), ())), preferred_element_type=F32)
            )
        for i, term in enumerate(terms):
            acc[i][...] = term if k == 0 else acc[i][...] + term
    for i, copy in enumerate(old):
        copy.wait()
        acc[i][...] += earlier[i][...]


def cuts_of(width):
    first = width % TILE or TILE
    sizes = [first // 2] * 2 if first == TILE else [first]
    sizes += [TILE] * ((width - first) // TILE)
    return [(sum(sizes[:i]), size) for i, size in enumerate(sizes)]


def chunk_matmul(scalars, half, recent, chunks, down, shrink, acc, sides, narrow, label, after=(), token=False):
    n = len(chunks[0][0])
    rows = chunks[0][0][0].shape[0] * n
    share = down.shape[1] // 2
    ranks = shrink.shape[0]
    spans = [(base, start, cuts_of(pieces[0].shape[1])) for pieces, base, start in chunks]
    sizes = [tile for _, _, cuts in spans for _, tile in cuts]
    width = sum(sizes)
    anywhere = pl.BlockSpec(memory_space=pl.ANY)
    held = [
        piece if i in late else in_hbm(piece)
        for pieces, base, _ in chunks
        for late in [recent[base > 0]]
        for i, piece in enumerate(pieces)
    ]
    args = [*after, *held, in_hbm(down), in_hbm(shrink), *(acc or ())]
    shapes = [(rows, share)] * len(sides) + [(ranks, rows)] * narrow
    marks = [(8, 128)] * token
    columns = share * len(sides) + ranks * narrow
    return pl.pallas_call(
        functools.partial(matmul_kernel, n, len(after), spans, half, sides, narrow, acc is not None, token),
        grid_spec=pltpu.PrefetchScalarGridSpec(
            num_scalar_prefetch=1,
            grid=(),
            in_specs=[anywhere] * len(args),
            out_specs=[pl.BlockSpec(memory_space=pltpu.VMEM)] * len(shapes + marks),
            scratch_shapes=[pltpu.VMEM((rows, tile), BF16) for tile in sizes]
            + [pltpu.VMEM((tile, share), BF16) for _ in sides for tile in sizes]
            + [pltpu.VMEM((ranks, tile), BF16) for tile in sizes if narrow]
            + [pltpu.VMEM(shape, F32) for shape in shapes if acc is not None]
            + [pltpu.SemaphoreType.DMA((len(sizes), n + 3)), pltpu.SemaphoreType.DMA((3,))],
        ),
        out_shape=[jax.ShapeDtypeStruct(shape, F32) for shape in shapes + marks],
        compiler_params=params(MATMUL_MIB),
        cost_estimate=pl.CostEstimate(
            flops=4 * rows * width * columns,
            bytes_accessed=2 * width * (columns + rows) + 8 * rows * columns,
            transcendentals=0,
        ),
        name=label,
    )(scalars, *args)


def final_kernel(n, owned, shrunk, slot, factors, kept, other, out, spread):
    rank = shrunk.shape[0]
    wide = owned * rank
    rows = out.shape[0]
    lane = lax.broadcasted_iota(jnp.int32, (rows, wide), 1) // rank
    own = shrunk[...].astype(F32).T
    pair = jnp.concatenate([own] * owned, axis=1)
    place = slot[...] - lane
    for i in range(n):
        spread[:, i * wide:(i + 1) * wide] = jnp.where(place == i * owned, pair, 0.0).astype(BF16)
    extra = jnp.dot(spread[...], factors[...], preferred_element_type=F32)
    out[...] = (kept[...] + other[...] + extra).astype(BF16)


def final(shrunk, slot_column, factors, kept, other, owned):
    n, wide, share = factors.shape
    rows = kept.shape[0]
    return pl.pallas_call(
        functools.partial(final_kernel, n, owned),
        in_specs=[pl.BlockSpec(memory_space=pltpu.VMEM)] * 5,
        out_specs=pl.BlockSpec(memory_space=pltpu.VMEM),
        scratch_shapes=[pltpu.VMEM((rows, n * wide), BF16)],
        out_shape=jax.ShapeDtypeStruct((rows, share), BF16),
        compiler_params=params(8),
        cost_estimate=pl.CostEstimate(
            flops=2 * rows * share * n * wide,
            bytes_accessed=2 * n * wide * share + 10 * rows * share,
            transcendentals=0,
        ),
        name="expand_and_add",
    )(shrunk, slot_column, factors.reshape(n * wide, share), kept, other)


def make_shards(n, cores):
    order = ring_order(n)
    place_of = {store: place for place, store in enumerate(order)}
    clockwise = [(order[i], order[(i + 1) % n]) for i in range(n)]
    counter = [(order[i], order[i - 1]) for i in range(n)]
    long, short = n // 2, (n - 1) // 2
    swap = [(t, (t + 1) % cores) for t in range(cores)]
    hops = [[0] + [-i for i in range(1, a + 1)] + list(range(1, b + 1)) for a, b in ((long, short), (short, long))]
    table = np.array(
        [
            [order[(place_of[s] + hop) % n] for way in hops for hop in way] + [t, 1 - t]
            for s in range(n)
            for t in range(cores)
        ],
        np.int32,
    )
    half = 2 * n

    def shards(hidden, down, shrink, expand, row_adapter, adapter_slot):
        owned, units, rank = shrink.shape
        store, tensor = lax.axis_index("store"), lax.axis_index("tensor")
        scalars = lax.dynamic_slice_in_dim(jnp.asarray(table), store * cores + tensor, 1, 0)[0]
        shrink_rows = jnp.transpose(shrink, (0, 2, 1)).reshape(owned * rank, units)

        slots = jnp.arange(adapter_slot.shape[0], dtype=jnp.int32)
        row_slot = jnp.sum(jnp.where(row_adapter[None, :] == slots[:, None], adapter_slot[:, None], 0), axis=0)

        width = units // CHUNKS
        blocks, mark = expand_blocks(scalars, half, expand, n, cores)

        def ring(chunk, own, holds):
            pieces = [own]
            for way, length in enumerate(lengths[chunk % 2]):
                moving = own
                for step in range(1, length + 1):
                    moving = lax.ppermute(moving, "store", (clockwise, counter)[way])
                    if (way, step) in holds:
                        moving = tie(moving, holds[way, step])
                    pieces.append(moving)
            return pieces, chunk % 2 * n, chunk * width

        def arrived(chunk, step):
            pieces, base, _ = chunk
            return [pieces[step], pieces[lengths[base > 0][0] + step]]

        lengths = ((long, short), (short, long))
        own = [hidden[:, chunk * width:(chunk + 1) * width] for chunk in range(CHUNKS)]
        own[-1] = tie(own[-1], [mark])
        first = [ring(chunk, own[chunk], {}) for chunk in range(2)]
        call = functools.partial(chunk_matmul, scalars, half)
        *acc, token = call(((long,), (n - 1,)), first, down, shrink_rows, None, (0, 1), True, "first_chunks", token=True)
        last = []
        for chunk in range(2):
            before = arrived(first[chunk], short)
            holds = {(0, 1): before, (1, 1): before, (chunk, short): [token]}
            last.append(ring(chunk + 2, own[chunk + 2], holds))
        ready = arrived(last[0], short) + arrived(last[1], short)
        factors = lax.all_to_all(tie(blocks, ready), "store", 0, 0)
        recent = ((short, long, n - 1), (short, n - 2, n - 1))
        call = functools.partial(call, recent)
        narrow, = call(last, down, shrink_rows, acc[2:], (), True, "last_narrow")
        mine = [
            jnp.where((row_slot == store * owned + i)[None, :], narrow[i * rank:(i + 1) * rank], 0.0)
            for i in range(owned)
        ]
        mine = sum(mine[1:], mine[0])
        send, = call(last, down, shrink_rows, acc[1:2], (1,), False, "last_sent", [mine])
        kept, = call(last, down, shrink_rows, acc[:1], (0,), False, "last_kept", [send])
        where = [(s, t) for s in range(n) for t in range(cores)]
        whole = mine
        for ds in range(2):
            for dt in range(cores):
                if ds or dt:
                    pairs = [(s * cores + t, (s ^ ds) * cores + (t + dt) % cores) for s, t in where]
                    whole = whole + lax.ppermute(mine, ("store", "tensor"), pairs)
        column = whole.astype(BF16)
        shrunk = column
        for ds in range(2, n, 2):
            shrunk = shrunk + lax.ppermute(column, "store", [(s, (s + ds) % n) for s in range(n)])
        other = lax.ppermute(send, "tensor", swap)
        return final(shrunk, row_slot[:, None], factors, kept, other, owned)

    return shards


def solution(mesh):
    in_specs = (
        P(("parts", "store"), "tensor"),
        P("tensor", "store"),
        P(("parts", "store"), "tensor", None),
        P(("parts", "store"), None, None),
        P("parts"),
        P("parts"),
    )
    out_specs = P("parts", ("store", "tensor"))
    shards = make_shards(mesh.shape["store"], mesh.shape["tensor"])
    return jax.shard_map(shards, mesh=mesh, in_specs=in_specs, out_specs=out_specs, check_vma=False)
```

```python
import functools

import jax
import jax.numpy as jnp
import numpy as np
from jax import lax
from jax.experimental import pallas as pl
from jax.experimental.pallas import tpu as pltpu
from jax.sharding import PartitionSpec as P

F32, BF16 = jnp.float32, jnp.bfloat16
TILE = 1024
CHUNKS = 4
MIB = 2**20


def params(mib):
    return pltpu.CompilerParams(vmem_limit_bytes=mib * MIB)


def in_hbm(array):
    return pltpu.with_memory_space_constraint(array, pltpu.HBM)


def ring_order(n):
    return list(range(0, n, 2)) + list(range(1, n, 2))[::-1]


def split_kernel(scalars, src, dst, mark):
    dst[...] = src[...][None]
    mark[...] = jnp.zeros_like(mark)


def expand_blocks(scalars, half, expand, n, cores):
    owned, rank, width = expand.shape
    rows = owned * rank
    share = width // (n * cores)
    return pl.pallas_call(
        split_kernel,
        grid_spec=pltpu.PrefetchScalarGridSpec(
            num_scalar_prefetch=1,
            grid=(n,),
            in_specs=[pl.BlockSpec((rows, share), lambda s, t: (0, s * cores + t[half]))],
            out_specs=[pl.BlockSpec((1, rows, share), lambda s, t: (s, 0, 0)), pl.BlockSpec((8, 128), lambda s, t: (0, 0))],
        ),
        out_shape=[jax.ShapeDtypeStruct((n, rows, share), BF16), jax.ShapeDtypeStruct((8, 128), F32)],
        compiler_params=params(4),
        cost_estimate=pl.CostEstimate(flops=0, bytes_accessed=4 * n * rows * share, transcendentals=0),
        name="expand_blocks",
    )(scalars, expand.reshape(rows, width))


def tie_kernel(*refs):
    pass


def tie(array, after):
    return pl.pallas_call(
        tie_kernel,
        in_specs=[pl.BlockSpec(memory_space=pl.ANY)] * (1 + len(after)),
        out_specs=pl.BlockSpec(memory_space=pl.ANY),
        out_shape=jax.ShapeDtypeStruct(array.shape, array.dtype),
        input_output_aliases={0: 0},
        compiler_params=params(1),
        name="tie",
    )(array, *after)


def matmul_kernel(n, waits, spans, half, sides, narrow, has_acc, scalars, *refs):
    refs = list(refs)[waits:]
    pieces = [[refs.pop(0) for _ in range(n)] for _ in spans]
    down = refs.pop(0)
    shrink = refs.pop(0)
    outs = len(sides) + narrow
    before = [refs.pop(0) for _ in range(outs)] if has_acc else []
    acc = [refs.pop(0) for _ in range(outs)]
    tiles = [(part, at, tile) for part, (_, _, cuts) in enumerate(spans) for at, tile in cuts]
    lefts = [refs.pop(0) for _ in tiles]
    weights = [[refs.pop(0) for _ in tiles] for _ in sides]
    ranks = [refs.pop(0) for _ in tiles] if narrow else []
    earlier = [refs.pop(0) for _ in before]
    sems, old_sems = refs
    rows = pieces[0][0].shape[0]
    share = down.shape[1] // 2

    copies = []
    for k, (part, at, tile) in enumerate(tiles):
        base, start, _ = spans[part]
        group = []
        for i in range(n):
            to = pl.multiple_of(scalars[base + i] * rows, rows)
            group.append((pieces[part][i].at[:, pl.ds(at, tile)], lefts[k].at[pl.ds(to, rows), :]))
        if narrow:
            group.append((shrink.at[:, pl.ds(start + at, tile)], ranks[k]))
        for i, side in enumerate(sides):
            column = pl.multiple_of(scalars[half + side] * share, share)
            group.append((down.at[pl.ds(start + at, tile), pl.ds(column, share)], weights[i][k]))
        copies.append([pltpu.make_async_copy(*pair, sems.at[k, i]) for i, pair in enumerate(group)])
        for copy in copies[-1]:
            copy.start()
    old = [pltpu.make_async_copy(a, b, old_sems.at[i]) for i, (a, b) in enumerate(zip(before, earlier))]
    for copy in old:
        copy.start()

    for k in range(len(tiles)):
        for copy in copies[k]:
            copy.wait()
        left = lefts[k][...]
        terms = [jnp.dot(left, weights[i][k][...], preferred_element_type=F32) for i in range(len(sides))]
        if narrow:
            terms.append(
                lax.dot_general(ranks[k][...], left, (((1,), (1,)), ((), ())), preferred_element_type=F32)
            )
        for i, term in enumerate(terms):
            acc[i][...] = term if k == 0 else acc[i][...] + term
    for i, copy in enumerate(old):
        copy.wait()
        acc[i][...] += earlier[i][...]


def cuts_of(width):
    first = width % TILE or TILE
    sizes = [first // 2] * 2 if first == TILE else [first]
    sizes += [TILE] * ((width - first) // TILE)
    return [(sum(sizes[:i]), size) for i, size in enumerate(sizes)]


def chunk_matmul(scalars, half, chunks, down, shrink, acc, sides, narrow, label, after=()):
    n = len(chunks[0][0])
    rows = chunks[0][0][0].shape[0] * n
    share = down.shape[1] // 2
    ranks = shrink.shape[0]
    spans = [(base, start, cuts_of(pieces[0].shape[1])) for pieces, base, start, _ in chunks]
    sizes = [tile for _, _, cuts in spans for _, tile in cuts]
    width = sum(sizes)
    anywhere = pl.BlockSpec(memory_space=pl.ANY)
    held = [
        piece if i in late else in_hbm(piece)
        for pieces, _, _, late in chunks
        for i, piece in enumerate(pieces)
    ]
    args = [*after, *held, in_hbm(down), in_hbm(shrink), *(acc or ())]
    shapes = [(rows, share)] * len(sides) + [(ranks, rows)] * narrow
    columns = share * len(sides) + ranks * narrow
    needed = 2 * width * (rows + columns) + (4 + 4 * (acc is not None)) * rows * columns
    return pl.pallas_call(
        functools.partial(matmul_kernel, n, len(after), spans, half, sides, narrow, acc is not None),
        grid_spec=pltpu.PrefetchScalarGridSpec(
            num_scalar_prefetch=1,
            grid=(),
            in_specs=[anywhere] * len(args),
            out_specs=[pl.BlockSpec(memory_space=pltpu.VMEM)] * len(shapes),
            scratch_shapes=[pltpu.VMEM((rows, tile), BF16) for tile in sizes]
            + [pltpu.VMEM((tile, share), BF16) for _ in sides for tile in sizes]
            + [pltpu.VMEM((ranks, tile), BF16) for tile in sizes if narrow]
            + [pltpu.VMEM(shape, F32) for shape in shapes if acc is not None]
            + [pltpu.SemaphoreType.DMA((len(sizes), n + 3)), pltpu.SemaphoreType.DMA((3,))],
        ),
        out_shape=[jax.ShapeDtypeStruct(shape, F32) for shape in shapes],
        compiler_params=params(-(-needed // MIB) + 4),
        cost_estimate=pl.CostEstimate(
            flops=4 * rows * width * columns,
            bytes_accessed=2 * width * (columns + rows) + 8 * rows * columns,
            transcendentals=0,
        ),
        name=label,
    )(scalars, *args)


def final_kernel(n, owned, shrunk, slot, factors, kept, other, out, spread):
    rank = shrunk.shape[0]
    wide = owned * rank
    rows = out.shape[0]
    lane = lax.broadcasted_iota(jnp.int32, (rows, wide), 1) // rank
    own = shrunk[...].astype(F32).T
    pair = jnp.concatenate([own] * owned, axis=1)
    place = slot[...] - lane
    for i in range(n):
        spread[:, i * wide:(i + 1) * wide] = jnp.where(place == i * owned, pair, 0.0).astype(BF16)
    extra = jnp.dot(spread[...], factors[...], preferred_element_type=F32)
    out[...] = (kept[...] + other[...] + extra).astype(BF16)


def final(shrunk, slot_column, factors, kept, other, owned):
    n, wide, share = factors.shape
    rows = kept.shape[0]
    return pl.pallas_call(
        functools.partial(final_kernel, n, owned),
        in_specs=[pl.BlockSpec(memory_space=pltpu.VMEM)] * 5,
        out_specs=pl.BlockSpec(memory_space=pltpu.VMEM),
        scratch_shapes=[pltpu.VMEM((rows, n * wide), BF16)],
        out_shape=jax.ShapeDtypeStruct((rows, share), BF16),
        compiler_params=params(8),
        cost_estimate=pl.CostEstimate(
            flops=2 * rows * share * n * wide,
            bytes_accessed=2 * n * wide * share + 10 * rows * share,
            transcendentals=0,
        ),
        name="expand_and_add",
    )(shrunk, slot_column, factors.reshape(n * wide, share), kept, other)


def make_shards(n, cores):
    order = ring_order(n)
    place_of = {store: place for place, store in enumerate(order)}
    clockwise = [(order[i], order[(i + 1) % n]) for i in range(n)]
    counter = [(order[i], order[i - 1]) for i in range(n)]
    long, short = n // 2, (n - 1) // 2
    swap = [(t, (t + 1) % cores) for t in range(cores)]
    hops = [[0] + [-i for i in range(1, a + 1)] + list(range(1, b + 1)) for a, b in ((long, short), (short, long))]
    table = np.array(
        [
            [order[(place_of[s] + hop) % n] for way in hops for hop in way] + [t, 1 - t]
            for s in range(n)
            for t in range(cores)
        ],
        np.int32,
    )
    half = 2 * n

    def shards(hidden, down, shrink, expand, row_adapter, adapter_slot):
        owned, units, rank = shrink.shape
        store, tensor = lax.axis_index("store"), lax.axis_index("tensor")
        scalars = lax.dynamic_slice_in_dim(jnp.asarray(table), store * cores + tensor, 1, 0)[0]
        shrink_rows = jnp.transpose(shrink, (0, 2, 1)).reshape(owned * rank, units)

        slots = jnp.arange(adapter_slot.shape[0], dtype=jnp.int32)
        row_slot = jnp.sum(jnp.where(row_adapter[None, :] == slots[:, None], adapter_slot[:, None], 0), axis=0)

        width = units // CHUNKS
        blocks, mark = expand_blocks(scalars, half, expand, n, cores)
        chunks, ends = [], []
        for chunk in range(CHUNKS):
            start = chunk * width
            own = hidden[:, start:start + width]
            if chunk == CHUNKS - 1:
                own = tie(own, [mark])
            way = chunk % 2
            pieces = [own]
            for length, pairs in zip(((long, short), (short, long))[way], (clockwise, counter)):
                moving = own
                for step in range(length):
                    moving = lax.ppermute(moving, "store", pairs)
                    pieces.append(moving)
                ends.append(moving)
            late = ((long,), (n - 1,)) if chunk < 2 else ((short, long, n - 1), (short, n - 2, n - 1))
            chunks.append((pieces, way * n, start, late[way]))
        factors = lax.all_to_all(tie(blocks, [ends[0], ends[3]]), "store", 0, 0)

        call = functools.partial(chunk_matmul, scalars, half)
        first, last = chunks[:CHUNKS // 2], chunks[CHUNKS // 2:]
        send, narrow = call(chunks, down, shrink_rows, None, (1,), True, "narrow_and_sent")
        mine = [
            jnp.where((row_slot == store * owned + i)[None, :], narrow[i * rank:(i + 1) * rank], 0.0)
            for i in range(owned)
        ]
        mine = sum(mine[1:], mine[0])
        kept = call(first, down, shrink_rows, None, (0,), False, "kept_first", [mine])
        where = [(s, t) for s in range(n) for t in range(cores)]
        whole = mine
        for ds in range(2):
            for dt in range(cores):
                if ds or dt:
                    pairs = [(s * cores + t, (s ^ ds) * cores + (t + dt) % cores) for s, t in where]
                    whole = whole + lax.ppermute(mine, ("store", "tensor"), pairs)
        column = whole.astype(BF16)
        kept, = call(last, down, shrink_rows, kept, (0,), False, "kept_last", [column])
        shrunk = column
        for ds in range(2, n, 2):
            shrunk = shrunk + lax.ppermute(column, "store", [(s, (s + ds) % n) for s in range(n)])
        other = lax.ppermute(send, "tensor", swap)
        return final(shrunk, row_slot[:, None], factors, kept, other, owned)

    return shards


def solution(mesh):
    in_specs = (
        P(("parts", "store"), "tensor"),
        P("tensor", "store"),
        P(("parts", "store"), "tensor", None),
        P(("parts", "store"), None, None),
        P("parts"),
        P("parts"),
    )
    out_specs = P("parts", ("store", "tensor"))
    shards = make_shards(mesh.shape["store"], mesh.shape["tensor"])
    return jax.shard_map(shards, mesh=mesh, in_specs=in_specs, out_specs=out_specs, check_vma=False)
```

```python
import functools

import jax
import jax.numpy as jnp
import numpy as np
from jax import lax
from jax.experimental import pallas as pl
from jax.experimental.pallas import tpu as pltpu
from jax.sharding import PartitionSpec as P

F32, BF16 = jnp.float32, jnp.bfloat16
TILE = 1024
CHUNKS = 4
MIB = 2**20
MATMUL_MIB = 28


def params(mib):
    return pltpu.CompilerParams(vmem_limit_bytes=mib * MIB)


def in_hbm(array):
    return pltpu.with_memory_space_constraint(array, pltpu.HBM)


def ring_order(n):
    return list(range(0, n, 2)) + list(range(1, n, 2))[::-1]


def split_kernel(scalars, src, dst, mark):
    dst[...] = src[...][None]
    mark[...] = jnp.zeros_like(mark)


def expand_blocks(scalars, half, expand, n, cores):
    owned, rank, width = expand.shape
    rows = owned * rank
    share = width // (n * cores)
    return pl.pallas_call(
        split_kernel,
        grid_spec=pltpu.PrefetchScalarGridSpec(
            num_scalar_prefetch=1,
            grid=(n,),
            in_specs=[pl.BlockSpec((rows, share), lambda s, t: (0, s * cores + t[half]))],
            out_specs=[pl.BlockSpec((1, rows, share), lambda s, t: (s, 0, 0)), pl.BlockSpec((8, 128), lambda s, t: (0, 0))],
        ),
        out_shape=[jax.ShapeDtypeStruct((n, rows, share), BF16), jax.ShapeDtypeStruct((8, 128), F32)],
        compiler_params=params(4),
        cost_estimate=pl.CostEstimate(flops=0, bytes_accessed=4 * n * rows * share, transcendentals=0),
        name="expand_blocks",
    )(scalars, expand.reshape(rows, width))


def tie_kernel(*refs):
    pass


def tie(array, after):
    return pl.pallas_call(
        tie_kernel,
        in_specs=[pl.BlockSpec(memory_space=pl.ANY)] * (1 + len(after)),
        out_specs=pl.BlockSpec(memory_space=pl.ANY),
        out_shape=jax.ShapeDtypeStruct(array.shape, array.dtype),
        input_output_aliases={0: 0},
        compiler_params=params(1),
        name="tie",
    )(array, *after)


def matmul_kernel(n, waits, spans, half, sides, narrow, has_acc, scalars, *refs):
    refs = list(refs)[waits:]
    pieces = [[refs.pop(0) for _ in range(n)] for _ in spans]
    down = refs.pop(0)
    shrink = refs.pop(0)
    outs = len(sides) + narrow
    before = [refs.pop(0) for _ in range(outs)] if has_acc else []
    acc = [refs.pop(0) for _ in range(outs)]
    tiles = [(part, at, tile) for part, (_, _, cuts) in enumerate(spans) for at, tile in cuts]
    lefts = [refs.pop(0) for _ in tiles]
    weights = [[refs.pop(0) for _ in tiles] for _ in sides]
    ranks = [refs.pop(0) for _ in tiles] if narrow else []
    earlier = [refs.pop(0) for _ in before]
    sems, old_sems = refs
    rows = pieces[0][0].shape[0]
    share = down.shape[1] // 2

    copies = []
    for k, (part, at, tile) in enumerate(tiles):
        base, start, _ = spans[part]
        group = []
        for i in range(n):
            to = pl.multiple_of(scalars[base + i] * rows, rows)
            group.append((pieces[part][i].at[:, pl.ds(at, tile)], lefts[k].at[pl.ds(to, rows), :]))
        if narrow:
            group.append((shrink.at[:, pl.ds(start + at, tile)], ranks[k]))
        for i, side in enumerate(sides):
            column = pl.multiple_of(scalars[half + side] * share, share)
            group.append((down.at[pl.ds(start + at, tile), pl.ds(column, share)], weights[i][k]))
        copies.append([pltpu.make_async_copy(*pair, sems.at[k, i]) for i, pair in enumerate(group)])
        for copy in copies[-1]:
            copy.start()
    old = [pltpu.make_async_copy(a, b, old_sems.at[i]) for i, (a, b) in enumerate(zip(before, earlier))]
    for copy in old:
        copy.start()

    for k in range(len(tiles)):
        for copy in copies[k]:
            copy.wait()
        left = lefts[k][...]
        terms = [jnp.dot(left, weights[i][k][...], preferred_element_type=F32) for i in range(len(sides))]
        if narrow:
            terms.append(
                lax.dot_general(ranks[k][...], left, (((1,), (1,)), ((), ())), preferred_element_type=F32)
            )
        for i, term in enumerate(terms):
            acc[i][...] = term if k == 0 else acc[i][...] + term
    for i, copy in enumerate(old):
        copy.wait()
        acc[i][...] += earlier[i][...]


def cuts_of(width):
    first = width % TILE or TILE
    sizes = [first // 2] * 2 if first == TILE else [first]
    sizes += [TILE] * ((width - first) // TILE)
    return [(sum(sizes[:i]), size) for i, size in enumerate(sizes)]


def chunk_matmul(scalars, half, chunks, down, shrink, acc, sides, narrow, label, after=()):
    n = len(chunks[0][0])
    rows = chunks[0][0][0].shape[0] * n
    share = down.shape[1] // 2
    ranks = shrink.shape[0]
    spans = [(base, start, cuts_of(pieces[0].shape[1])) for pieces, base, start, _ in chunks]
    sizes = [tile for _, _, cuts in spans for _, tile in cuts]
    width = sum(sizes)
    anywhere = pl.BlockSpec(memory_space=pl.ANY)
    held = [
        piece if i in late else in_hbm(piece)
        for pieces, _, _, late in chunks
        for i, piece in enumerate(pieces)
    ]
    args = [*after, *held, in_hbm(down), in_hbm(shrink), *(acc or ())]
    shapes = [(rows, share)] * len(sides) + [(ranks, rows)] * narrow
    columns = share * len(sides) + ranks * narrow
    return pl.pallas_call(
        functools.partial(matmul_kernel, n, len(after), spans, half, sides, narrow, acc is not None),
        grid_spec=pltpu.PrefetchScalarGridSpec(
            num_scalar_prefetch=1,
            grid=(),
            in_specs=[anywhere] * len(args),
            out_specs=[pl.BlockSpec(memory_space=pltpu.VMEM)] * len(shapes),
            scratch_shapes=[pltpu.VMEM((rows, tile), BF16) for tile in sizes]
            + [pltpu.VMEM((tile, share), BF16) for _ in sides for tile in sizes]
            + [pltpu.VMEM((ranks, tile), BF16) for tile in sizes if narrow]
            + [pltpu.VMEM(shape, F32) for shape in shapes if acc is not None]
            + [pltpu.SemaphoreType.DMA((len(sizes), n + 3)), pltpu.SemaphoreType.DMA((3,))],
        ),
        out_shape=[jax.ShapeDtypeStruct(shape, F32) for shape in shapes],
        compiler_params=params(MATMUL_MIB),
        cost_estimate=pl.CostEstimate(
            flops=4 * rows * width * columns,
            bytes_accessed=2 * width * (columns + rows) + 8 * rows * columns,
            transcendentals=0,
        ),
        name=label,
    )(scalars, *args)


def final_kernel(n, owned, shrunk, slot, factors, kept, other, out, spread, factors_here, kept_here, other_here, sems):
    pairs = [(factors, factors_here), (kept, kept_here), (other, other_here)]
    copies = [pltpu.make_async_copy(a, b, sems.at[i]) for i, (a, b) in enumerate(pairs)]
    for copy in copies:
        copy.start()
    rank = shrunk.shape[0]
    wide = owned * rank
    rows = out.shape[0]
    lane = lax.broadcasted_iota(jnp.int32, (rows, wide), 1) // rank
    own = shrunk[...].astype(F32).T
    pair = jnp.concatenate([own] * owned, axis=1)
    place = slot[...] - lane
    for i in range(n):
        spread[:, i * wide:(i + 1) * wide] = jnp.where(place == i * owned, pair, 0.0).astype(BF16)
    copies[0].wait()
    extra = jnp.dot(spread[...], factors_here[...], preferred_element_type=F32)
    copies[1].wait()
    copies[2].wait()
    out[...] = (kept_here[...] + other_here[...] + extra).astype(BF16)


def final(shrunk, slot_column, factors, kept, other, owned):
    n, wide, share = factors.shape
    rows = kept.shape[0]
    return pl.pallas_call(
        functools.partial(final_kernel, n, owned),
        in_specs=[pl.BlockSpec(memory_space=pltpu.VMEM)] * 2 + [pl.BlockSpec(memory_space=pl.ANY)] * 3,
        out_specs=pl.BlockSpec(memory_space=pltpu.VMEM),
        scratch_shapes=[
            pltpu.VMEM((rows, n * wide), BF16),
            pltpu.VMEM((n * wide, share), BF16),
            pltpu.VMEM((rows, share), F32),
            pltpu.VMEM((rows, share), F32),
            pltpu.SemaphoreType.DMA((3,)),
        ],
        out_shape=jax.ShapeDtypeStruct((rows, share), BF16),
        compiler_params=params(16),
        cost_estimate=pl.CostEstimate(
            flops=2 * rows * share * n * wide,
            bytes_accessed=2 * n * wide * share + 10 * rows * share,
            transcendentals=0,
        ),
        name="expand_and_add",
    )(shrunk, slot_column, in_hbm(factors.reshape(n * wide, share)), kept, other)


def make_shards(n, cores):
    order = ring_order(n)
    place_of = {store: place for place, store in enumerate(order)}
    clockwise = [(order[i], order[(i + 1) % n]) for i in range(n)]
    counter = [(order[i], order[i - 1]) for i in range(n)]
    long, short = n // 2, (n - 1) // 2
    swap = [(t, (t + 1) % cores) for t in range(cores)]
    hops = [[0] + [-i for i in range(1, a + 1)] + list(range(1, b + 1)) for a, b in ((long, short), (short, long))]
    table = np.array(
        [
            [order[(place_of[s] + hop) % n] for way in hops for hop in way] + [t, 1 - t]
            for s in range(n)
            for t in range(cores)
        ],
        np.int32,
    )
    half = 2 * n

    def shards(hidden, down, shrink, expand, row_adapter, adapter_slot):
        owned, units, rank = shrink.shape
        store, tensor = lax.axis_index("store"), lax.axis_index("tensor")
        scalars = lax.dynamic_slice_in_dim(jnp.asarray(table), store * cores + tensor, 1, 0)[0]
        shrink_rows = jnp.transpose(shrink, (0, 2, 1)).reshape(owned * rank, units)

        slots = jnp.arange(adapter_slot.shape[0], dtype=jnp.int32)
        row_slot = jnp.sum(jnp.where(row_adapter[None, :] == slots[:, None], adapter_slot[:, None], 0), axis=0)

        width = units // CHUNKS
        blocks, mark = expand_blocks(scalars, half, expand, n, cores)
        chunks, ends = [], []
        for chunk in range(CHUNKS):
            start = chunk * width
            own = hidden[:, start:start + width]
            if chunk == CHUNKS - 1:
                own = tie(own, [mark])
            way = chunk % 2
            pieces = [own]
            for length, pairs in zip(((long, short), (short, long))[way], (clockwise, counter)):
                moving = own
                for step in range(length):
                    moving = lax.ppermute(moving, "store", pairs)
                    pieces.append(moving)
                ends.append(moving)
            late = ((long,), (n - 1,)) if chunk < 2 else ((short, long, n - 1), (short, n - 2, n - 1))
            chunks.append((pieces, way * n, start, late[way]))
        factors = lax.all_to_all(tie(blocks, [ends[0], ends[3]]), "store", 0, 0)

        call = functools.partial(chunk_matmul, scalars, half)
        first, last = chunks[:CHUNKS // 2], chunks[CHUNKS // 2:]
        acc = call(first, down, shrink_rows, None, (0, 1), True, "first_chunks")
        narrow, = call(last, down, shrink_rows, acc[2:], (), True, "last_narrow")
        mine = [
            jnp.where((row_slot == store * owned + i)[None, :], narrow[i * rank:(i + 1) * rank], 0.0)
            for i in range(owned)
        ]
        mine = sum(mine[1:], mine[0])
        send, = call(last, down, shrink_rows, acc[1:2], (1,), False, "last_sent", [mine])
        kept, = call(last, down, shrink_rows, acc[:1], (0,), False, "last_kept", [send])
        where = [(s, t) for s in range(n) for t in range(cores)]
        whole = mine
        for ds in range(2):
            for dt in range(cores):
                if ds or dt:
                    pairs = [(s * cores + t, (s ^ ds) * cores + (t + dt) % cores) for s, t in where]
                    whole = whole + lax.ppermute(mine, ("store", "tensor"), pairs)
        column = whole.astype(BF16)
        shrunk = column
        for ds in range(2, n, 2):
            shrunk = shrunk + lax.ppermute(column, "store", [(s, (s + ds) % n) for s in range(n)])
        other = lax.ppermute(send, "tensor", swap)
        return final(shrunk, row_slot[:, None], factors, kept, other, owned)

    return shards


def solution(mesh):
    in_specs = (
        P(("parts", "store"), "tensor"),
        P("tensor", "store"),
        P(("parts", "store"), "tensor", None),
        P(("parts", "store"), None, None),
        P("parts"),
        P("parts"),
    )
    out_specs = P("parts", ("store", "tensor"))
    shards = make_shards(mesh.shape["store"], mesh.shape["tensor"])
    return jax.shard_map(shards, mesh=mesh, in_specs=in_specs, out_specs=out_specs, check_vma=False)
```

```python
import functools

import jax
import jax.numpy as jnp
import numpy as np
from jax import lax
from jax.experimental import pallas as pl
from jax.experimental.pallas import tpu as pltpu
from jax.sharding import PartitionSpec as P

F32, BF16 = jnp.float32, jnp.bfloat16
TILE = 1024
CHUNKS = 4
MIB = 2**20
MATMUL_MIB = 28


def params(mib):
    return pltpu.CompilerParams(vmem_limit_bytes=mib * MIB)


def in_hbm(array):
    return pltpu.with_memory_space_constraint(array, pltpu.HBM)


def ring_order(n):
    return list(range(0, n, 2)) + list(range(1, n, 2))[::-1]


def split_kernel(scalars, src, dst, mark):
    dst[...] = src[...][None]
    mark[...] = jnp.zeros_like(mark)


def expand_blocks(scalars, half, expand, n, cores):
    owned, rank, width = expand.shape
    rows = owned * rank
    share = width // (n * cores)
    return pl.pallas_call(
        split_kernel,
        grid_spec=pltpu.PrefetchScalarGridSpec(
            num_scalar_prefetch=1,
            grid=(n,),
            in_specs=[pl.BlockSpec((rows, share), lambda s, t: (0, s * cores + t[half]))],
            out_specs=[pl.BlockSpec((1, rows, share), lambda s, t: (s, 0, 0)), pl.BlockSpec((8, 128), lambda s, t: (0, 0))],
        ),
        out_shape=[jax.ShapeDtypeStruct((n, rows, share), BF16), jax.ShapeDtypeStruct((8, 128), F32)],
        compiler_params=params(4),
        cost_estimate=pl.CostEstimate(flops=0, bytes_accessed=4 * n * rows * share, transcendentals=0),
        name="expand_blocks",
    )(scalars, expand.reshape(rows, width))


def tie_kernel(*refs):
    pass


def tie(array, after):
    return pl.pallas_call(
        tie_kernel,
        in_specs=[pl.BlockSpec(memory_space=pl.ANY)] * (1 + len(after)),
        out_specs=pl.BlockSpec(memory_space=pl.ANY),
        out_shape=jax.ShapeDtypeStruct(array.shape, array.dtype),
        input_output_aliases={0: 0},
        compiler_params=params(1),
        name="tie",
    )(array, *after)


def matmul_kernel(n, waits, spans, half, sides, narrow, has_acc, scalars, *refs):
    refs = list(refs)[waits:]
    pieces = [[refs.pop(0) for _ in range(n)] for _ in spans]
    down = refs.pop(0)
    shrink = refs.pop(0)
    outs = len(sides) + narrow
    before = [refs.pop(0) for _ in range(outs)] if has_acc else []
    acc = [refs.pop(0) for _ in range(outs)]
    tiles = [(part, at, tile) for part, (_, _, cuts) in enumerate(spans) for at, tile in cuts]
    lefts = [refs.pop(0) for _ in tiles]
    weights = [[refs.pop(0) for _ in tiles] for _ in sides]
    ranks = [refs.pop(0) for _ in tiles] if narrow else []
    earlier = [refs.pop(0) for _ in before]
    sems, old_sems = refs
    rows = pieces[0][0].shape[0]
    share = down.shape[1] // 2

    copies = []
    for k, (part, at, tile) in enumerate(tiles):
        base, start, _ = spans[part]
        group = []
        for i in range(n):
            to = pl.multiple_of(scalars[base + i] * rows, rows)
            group.append((pieces[part][i].at[:, pl.ds(at, tile)], lefts[k].at[pl.ds(to, rows), :]))
        if narrow:
            group.append((shrink.at[:, pl.ds(start + at, tile)], ranks[k]))
        for i, side in enumerate(sides):
            column = pl.multiple_of(scalars[half + side] * share, share)
            group.append((down.at[pl.ds(start + at, tile), pl.ds(column, share)], weights[i][k]))
        copies.append([pltpu.make_async_copy(*pair, sems.at[k, i]) for i, pair in enumerate(group)])
        for copy in copies[-1]:
            copy.start()
    old = [pltpu.make_async_copy(a, b, old_sems.at[i]) for i, (a, b) in enumerate(zip(before, earlier))]
    for copy in old:
        copy.start()

    for k in range(len(tiles)):
        for copy in copies[k]:
            copy.wait()
        left = lefts[k][...]
        terms = [jnp.dot(left, weights[i][k][...], preferred_element_type=F32) for i in range(len(sides))]
        if narrow:
            terms.append(
                lax.dot_general(ranks[k][...], left, (((1,), (1,)), ((), ())), preferred_element_type=F32)
            )
        for i, term in enumerate(terms):
            acc[i][...] = term if k == 0 else acc[i][...] + term
    for i, copy in enumerate(old):
        copy.wait()
        acc[i][...] += earlier[i][...]


def cuts_of(width):
    first = width % TILE or TILE
    sizes = [first // 2] * 2 if first == TILE else [first]
    sizes += [TILE] * ((width - first) // TILE)
    return [(sum(sizes[:i]), size) for i, size in enumerate(sizes)]


def chunk_matmul(scalars, half, chunks, down, shrink, acc, sides, narrow, label, after=()):
    n = len(chunks[0][0])
    rows = chunks[0][0][0].shape[0] * n
    share = down.shape[1] // 2
    ranks = shrink.shape[0]
    spans = [(base, start, cuts_of(pieces[0].shape[1])) for pieces, base, start, _ in chunks]
    sizes = [tile for _, _, cuts in spans for _, tile in cuts]
    width = sum(sizes)
    anywhere = pl.BlockSpec(memory_space=pl.ANY)
    held = [
        piece if i in late else in_hbm(piece)
        for pieces, _, _, late in chunks
        for i, piece in enumerate(pieces)
    ]
    args = [*after, *held, in_hbm(down), in_hbm(shrink), *(acc or ())]
    shapes = [(rows, share)] * len(sides) + [(ranks, rows)] * narrow
    columns = share * len(sides) + ranks * narrow
    return pl.pallas_call(
        functools.partial(matmul_kernel, n, len(after), spans, half, sides, narrow, acc is not None),
        grid_spec=pltpu.PrefetchScalarGridSpec(
            num_scalar_prefetch=1,
            grid=(),
            in_specs=[anywhere] * len(args),
            out_specs=[pl.BlockSpec(memory_space=pltpu.VMEM)] * len(shapes),
            scratch_shapes=[pltpu.VMEM((rows, tile), BF16) for tile in sizes]
            + [pltpu.VMEM((tile, share), BF16) for _ in sides for tile in sizes]
            + [pltpu.VMEM((ranks, tile), BF16) for tile in sizes if narrow]
            + [pltpu.VMEM(shape, F32) for shape in shapes if acc is not None]
            + [pltpu.SemaphoreType.DMA((len(sizes), n + 3)), pltpu.SemaphoreType.DMA((3,))],
        ),
        out_shape=[jax.ShapeDtypeStruct(shape, F32) for shape in shapes],
        compiler_params=params(MATMUL_MIB),
        cost_estimate=pl.CostEstimate(
            flops=4 * rows * width * columns,
            bytes_accessed=2 * width * (columns + rows) + 8 * rows * columns,
            transcendentals=0,
        ),
        name=label,
    )(scalars, *args)


def final_kernel(n, owned, shrunk, slot, factors, kept, other, out, spread):
    rank = shrunk.shape[0]
    wide = owned * rank
    rows = out.shape[0]
    lane = lax.broadcasted_iota(jnp.int32, (rows, wide), 1) // rank
    own = shrunk[...].astype(F32).T
    pair = jnp.concatenate([own] * owned, axis=1)
    place = slot[...] - lane
    for i in range(n):
        spread[:, i * wide:(i + 1) * wide] = jnp.where(place == i * owned, pair, 0.0).astype(BF16)
    extra = jnp.dot(spread[...], factors[...], preferred_element_type=F32)
    out[...] = (kept[...] + other[...] + extra).astype(BF16)


def final(shrunk, slot_column, factors, kept, other, owned):
    n, wide, share = factors.shape
    rows = kept.shape[0]
    return pl.pallas_call(
        functools.partial(final_kernel, n, owned),
        in_specs=[pl.BlockSpec(memory_space=pltpu.VMEM)] * 5,
        out_specs=pl.BlockSpec(memory_space=pltpu.VMEM),
        scratch_shapes=[pltpu.VMEM((rows, n * wide), BF16)],
        out_shape=jax.ShapeDtypeStruct((rows, share), BF16),
        compiler_params=params(8),
        cost_estimate=pl.CostEstimate(
            flops=2 * rows * share * n * wide,
            bytes_accessed=2 * n * wide * share + 10 * rows * share,
            transcendentals=0,
        ),
        name="expand_and_add",
    )(shrunk, slot_column, factors.reshape(n * wide, share), kept, other)


def make_shards(n, cores):
    order = ring_order(n)
    place_of = {store: place for place, store in enumerate(order)}
    clockwise = [(order[i], order[(i + 1) % n]) for i in range(n)]
    counter = [(order[i], order[i - 1]) for i in range(n)]
    long, short = n // 2, (n - 1) // 2
    swap = [(t, (t + 1) % cores) for t in range(cores)]
    hops = [[0] + [-i for i in range(1, a + 1)] + list(range(1, b + 1)) for a, b in ((long, short), (short, long))]
    table = np.array(
        [
            [order[(place_of[s] + hop) % n] for way in hops for hop in way] + [t, 1 - t]
            for s in range(n)
            for t in range(cores)
        ],
        np.int32,
    )
    half = 2 * n

    def shards(hidden, down, shrink, expand, row_adapter, adapter_slot):
        owned, units, rank = shrink.shape
        store, tensor = lax.axis_index("store"), lax.axis_index("tensor")
        scalars = lax.dynamic_slice_in_dim(jnp.asarray(table), store * cores + tensor, 1, 0)[0]
        shrink_rows = jnp.transpose(shrink, (0, 2, 1)).reshape(owned * rank, units)

        slots = jnp.arange(adapter_slot.shape[0], dtype=jnp.int32)
        row_slot = jnp.sum(jnp.where(row_adapter[None, :] == slots[:, None], adapter_slot[:, None], 0), axis=0)

        width = units // CHUNKS
        blocks, mark = expand_blocks(scalars, half, expand, n, cores)
        chunks, ends = [], []
        for chunk in range(CHUNKS):
            start = chunk * width
            own = hidden[:, start:start + width]
            if chunk == CHUNKS - 1:
                own = tie(own, [mark])
            way = chunk % 2
            pieces = [own]
            for length, pairs in zip(((long, short), (short, long))[way], (clockwise, counter)):
                moving = own
                for step in range(length):
                    moving = lax.ppermute(moving, "store", pairs)
                    pieces.append(moving)
                ends.append(moving)
            late = ((long,), (n - 1,)) if chunk < 2 else ((short, long, n - 1), (short, n - 2, n - 1))
            chunks.append((pieces, way * n, start, late[way]))
        factors = lax.all_to_all(tie(blocks, [ends[0], ends[3], ends[5], ends[6]]), "store", 0, 0)

        call = functools.partial(chunk_matmul, scalars, half)
        first, last = chunks[:CHUNKS // 2], chunks[CHUNKS // 2:]
        acc = call(first, down, shrink_rows, None, (0, 1), True, "first_chunks")
        narrow, = call(last, down, shrink_rows, acc[2:], (), True, "last_narrow")
        mine = [
            jnp.where((row_slot == store * owned + i)[None, :], narrow[i * rank:(i + 1) * rank], 0.0)
            for i in range(owned)
        ]
        mine = sum(mine[1:], mine[0])
        send, = call(last, down, shrink_rows, acc[1:2], (1,), False, "last_sent", [mine])
        kept, = call(last, down, shrink_rows, acc[:1], (0,), False, "last_kept", [send])
        where = [(s, t) for s in range(n) for t in range(cores)]
        whole = mine
        for ds in range(2):
            for dt in range(cores):
                if ds or dt:
                    pairs = [(s * cores + t, (s ^ ds) * cores + (t + dt) % cores) for s, t in where]
                    whole = whole + lax.ppermute(mine, ("store", "tensor"), pairs)
        column = whole.astype(BF16)
        shrunk = column
        for ds in range(2, n, 2):
            shrunk = shrunk + lax.ppermute(column, "store", [(s, (s + ds) % n) for s in range(n)])
        other = lax.ppermute(send, "tensor", swap)
        return final(shrunk, row_slot[:, None], factors, kept, other, owned)

    return shards


def solution(mesh):
    in_specs = (
        P(("parts", "store"), "tensor"),
        P("tensor", "store"),
        P(("parts", "store"), "tensor", None),
        P(("parts", "store"), None, None),
        P("parts"),
        P("parts"),
    )
    out_specs = P("parts", ("store", "tensor"))
    shards = make_shards(mesh.shape["store"], mesh.shape["tensor"])
    return jax.shard_map(shards, mesh=mesh, in_specs=in_specs, out_specs=out_specs, check_vma=False)
```

```python
import functools

import jax
import jax.numpy as jnp
import numpy as np
from jax import lax
from jax.experimental import pallas as pl
from jax.experimental.pallas import tpu as pltpu
from jax.sharding import PartitionSpec as P

F32, BF16 = jnp.float32, jnp.bfloat16
TILE = 1024
CHUNKS = 4
MIB = 2**20
MATMUL_MIB = 28


def params(mib):
    return pltpu.CompilerParams(vmem_limit_bytes=mib * MIB)


def in_hbm(array):
    return pltpu.with_memory_space_constraint(array, pltpu.HBM)


def ring_order(n):
    return list(range(0, n, 2)) + list(range(1, n, 2))[::-1]


def split_kernel(scalars, src, dst, mark):
    dst[...] = src[...][None]
    mark[...] = jnp.zeros_like(mark)


def expand_blocks(scalars, half, expand, n, cores):
    owned, rank, width = expand.shape
    rows = owned * rank
    share = width // (n * cores)
    return pl.pallas_call(
        split_kernel,
        grid_spec=pltpu.PrefetchScalarGridSpec(
            num_scalar_prefetch=1,
            grid=(n,),
            in_specs=[pl.BlockSpec((rows, share), lambda s, t: (0, s * cores + t[half]))],
            out_specs=[pl.BlockSpec((1, rows, share), lambda s, t: (s, 0, 0)), pl.BlockSpec((8, 128), lambda s, t: (0, 0))],
        ),
        out_shape=[jax.ShapeDtypeStruct((n, rows, share), BF16), jax.ShapeDtypeStruct((8, 128), F32)],
        compiler_params=params(4),
        cost_estimate=pl.CostEstimate(flops=0, bytes_accessed=4 * n * rows * share, transcendentals=0),
        name="expand_blocks",
    )(scalars, expand.reshape(rows, width))


def tie_kernel(*refs):
    pass


def tie(array, after):
    return pl.pallas_call(
        tie_kernel,
        in_specs=[pl.BlockSpec(memory_space=pl.ANY)] * (1 + len(after)),
        out_specs=pl.BlockSpec(memory_space=pl.ANY),
        out_shape=jax.ShapeDtypeStruct(array.shape, array.dtype),
        input_output_aliases={0: 0},
        compiler_params=params(1),
        name="tie",
    )(array, *after)


def matmul_kernel(n, waits, spans, half, sides, narrow, has_acc, scalars, *refs):
    refs = list(refs)[waits:]
    pieces = [[refs.pop(0) for _ in range(n)] for _ in spans]
    down = refs.pop(0)
    shrink = refs.pop(0)
    outs = len(sides) + narrow
    before = [refs.pop(0) for _ in range(outs)] if has_acc else []
    acc = [refs.pop(0) for _ in range(outs)]
    tiles = [(part, at, tile) for part, (_, _, cuts) in enumerate(spans) for at, tile in cuts]
    lefts = [refs.pop(0) for _ in tiles]
    weights = [[refs.pop(0) for _ in tiles] for _ in sides]
    ranks = [refs.pop(0) for _ in tiles] if narrow else []
    earlier = [refs.pop(0) for _ in before]
    sems, old_sems = refs
    rows = pieces[0][0].shape[0]
    share = down.shape[1] // 2

    copies = []
    for k, (part, at, tile) in enumerate(tiles):
        base, start, _ = spans[part]
        group = []
        for i in range(n):
            to = pl.multiple_of(scalars[base + i] * rows, rows)
            group.append((pieces[part][i].at[:, pl.ds(at, tile)], lefts[k].at[pl.ds(to, rows), :]))
        if narrow:
            group.append((shrink.at[:, pl.ds(start + at, tile)], ranks[k]))
        for i, side in enumerate(sides):
            column = pl.multiple_of(scalars[half + side] * share, share)
            group.append((down.at[pl.ds(start + at, tile), pl.ds(column, share)], weights[i][k]))
        copies.append([pltpu.make_async_copy(*pair, sems.at[k, i]) for i, pair in enumerate(group)])
        for copy in copies[-1]:
            copy.start()
    old = [pltpu.make_async_copy(a, b, old_sems.at[i]) for i, (a, b) in enumerate(zip(before, earlier))]
    for copy in old:
        copy.start()

    for k in range(len(tiles)):
        for copy in copies[k]:
            copy.wait()
        left = lefts[k][...]
        terms = [jnp.dot(left, weights[i][k][...], preferred_element_type=F32) for i in range(len(sides))]
        if narrow:
            terms.append(
                lax.dot_general(ranks[k][...], left, (((1,), (1,)), ((), ())), preferred_element_type=F32)
            )
        for i, term in enumerate(terms):
            acc[i][...] = term if k == 0 else acc[i][...] + term
    for i, copy in enumerate(old):
        copy.wait()
        acc[i][...] += earlier[i][...]


def cuts_of(width):
    first = width % TILE or TILE
    sizes = [first // 2] * 2 if first == TILE else [first]
    sizes += [TILE] * ((width - first) // TILE)
    return [(sum(sizes[:i]), size) for i, size in enumerate(sizes)]


def chunk_matmul(scalars, half, chunks, down, shrink, acc, sides, narrow, label, after=()):
    n = len(chunks[0][0])
    rows = chunks[0][0][0].shape[0] * n
    share = down.shape[1] // 2
    ranks = shrink.shape[0]
    spans = [(base, start, cuts_of(pieces[0].shape[1])) for pieces, base, start, _ in chunks]
    sizes = [tile for _, _, cuts in spans for _, tile in cuts]
    width = sum(sizes)
    anywhere = pl.BlockSpec(memory_space=pl.ANY)
    held = [
        piece if i in late else in_hbm(piece)
        for pieces, _, _, late in chunks
        for i, piece in enumerate(pieces)
    ]
    args = [*after, *held, in_hbm(down), in_hbm(shrink), *(acc or ())]
    shapes = [(rows, share)] * len(sides) + [(ranks, rows)] * narrow
    columns = share * len(sides) + ranks * narrow
    return pl.pallas_call(
        functools.partial(matmul_kernel, n, len(after), spans, half, sides, narrow, acc is not None),
        grid_spec=pltpu.PrefetchScalarGridSpec(
            num_scalar_prefetch=1,
            grid=(),
            in_specs=[anywhere] * len(args),
            out_specs=[pl.BlockSpec(memory_space=pltpu.VMEM)] * len(shapes),
            scratch_shapes=[pltpu.VMEM((rows, tile), BF16) for tile in sizes]
            + [pltpu.VMEM((tile, share), BF16) for _ in sides for tile in sizes]
            + [pltpu.VMEM((ranks, tile), BF16) for tile in sizes if narrow]
            + [pltpu.VMEM(shape, F32) for shape in shapes if acc is not None]
            + [pltpu.SemaphoreType.DMA((len(sizes), n + 3)), pltpu.SemaphoreType.DMA((3,))],
        ),
        out_shape=[jax.ShapeDtypeStruct(shape, F32) for shape in shapes],
        compiler_params=params(MATMUL_MIB),
        cost_estimate=pl.CostEstimate(
            flops=4 * rows * width * columns,
            bytes_accessed=2 * width * (columns + rows) + 8 * rows * columns,
            transcendentals=0,
        ),
        name=label,
    )(scalars, *args)


def final_kernel(n, owned, shrunk, slot, factors, kept, other, out, spread):
    rank = shrunk.shape[0]
    wide = owned * rank
    rows = out.shape[0]
    lane = lax.broadcasted_iota(jnp.int32, (rows, wide), 1) // rank
    own = shrunk[...].astype(F32).T
    pair = jnp.concatenate([own] * owned, axis=1)
    place = slot[...] - lane
    for i in range(n):
        spread[:, i * wide:(i + 1) * wide] = jnp.where(place == i * owned, pair, 0.0).astype(BF16)
    extra = jnp.dot(spread[...], factors[...], preferred_element_type=F32)
    out[...] = (kept[...] + other[...] + extra).astype(BF16)


def final(shrunk, slot_column, factors, kept, other, owned):
    n, wide, share = factors.shape
    rows = kept.shape[0]
    return pl.pallas_call(
        functools.partial(final_kernel, n, owned),
        in_specs=[pl.BlockSpec(memory_space=pltpu.VMEM)] * 5,
        out_specs=pl.BlockSpec(memory_space=pltpu.VMEM),
        scratch_shapes=[pltpu.VMEM((rows, n * wide), BF16)],
        out_shape=jax.ShapeDtypeStruct((rows, share), BF16),
        compiler_params=params(8),
        cost_estimate=pl.CostEstimate(
            flops=2 * rows * share * n * wide,
            bytes_accessed=2 * n * wide * share + 10 * rows * share,
            transcendentals=0,
        ),
        name="expand_and_add",
    )(shrunk, slot_column, factors.reshape(n * wide, share), kept, other)


def make_shards(n, cores):
    order = ring_order(n)
    place_of = {store: place for place, store in enumerate(order)}
    clockwise = [(order[i], order[(i + 1) % n]) for i in range(n)]
    counter = [(order[i], order[i - 1]) for i in range(n)]
    long, short = n // 2, (n - 1) // 2
    swap = [(t, (t + 1) % cores) for t in range(cores)]
    hops = [[0] + [-i for i in range(1, a + 1)] + list(range(1, b + 1)) for a, b in ((long, short), (short, long))]
    table = np.array(
        [
            [order[(place_of[s] + hop) % n] for way in hops for hop in way] + [t, 1 - t]
            for s in range(n)
            for t in range(cores)
        ],
        np.int32,
    )
    half = 2 * n

    def shards(hidden, down, shrink, expand, row_adapter, adapter_slot):
        owned, units, rank = shrink.shape
        store, tensor = lax.axis_index("store"), lax.axis_index("tensor")
        scalars = lax.dynamic_slice_in_dim(jnp.asarray(table), store * cores + tensor, 1, 0)[0]
        shrink_rows = jnp.transpose(shrink, (0, 2, 1)).reshape(owned * rank, units)

        slots = jnp.arange(adapter_slot.shape[0], dtype=jnp.int32)
        row_slot = jnp.sum(jnp.where(row_adapter[None, :] == slots[:, None], adapter_slot[:, None], 0), axis=0)

        width = units // CHUNKS
        blocks, mark = expand_blocks(scalars, half, expand, n, cores)
        chunks, ends = [], []
        for chunk in range(CHUNKS):
            start = chunk * width
            own = hidden[:, start:start + width]
            if chunk == CHUNKS - 1:
                own = tie(own, [mark])
            way = chunk % 2
            pieces = [own]
            for length, pairs in zip(((long, short), (short, long))[way], (clockwise, counter)):
                moving = own
                for step in range(length):
                    moving = lax.ppermute(moving, "store", pairs)
                    pieces.append(moving)
                ends.append(moving)
            late = ((long,), (n - 1,)) if chunk < 2 else ((short, long, n - 1), (short, n - 2, n - 1))
            chunks.append((pieces, way * n, start, late[way]))
        factors = lax.all_to_all(tie(blocks, ends[:4]), "store", 0, 0)

        call = functools.partial(chunk_matmul, scalars, half)
        first, last = chunks[:CHUNKS // 2], chunks[CHUNKS // 2:]
        acc = call(first, down, shrink_rows, None, (0, 1), True, "first_chunks")
        narrow, = call(last, down, shrink_rows, acc[2:], (), True, "last_narrow")
        mine = [
            jnp.where((row_slot == store * owned + i)[None, :], narrow[i * rank:(i + 1) * rank], 0.0)
            for i in range(owned)
        ]
        mine = sum(mine[1:], mine[0])
        send, = call(last, down, shrink_rows, acc[1:2], (1,), False, "last_sent", [mine])
        kept, = call(last, down, shrink_rows, acc[:1], (0,), False, "last_kept", [send])
        where = [(s, t) for s in range(n) for t in range(cores)]
        whole = mine
        for ds in range(2):
            for dt in range(cores):
                if ds or dt:
                    pairs = [(s * cores + t, (s ^ ds) * cores + (t + dt) % cores) for s, t in where]
                    whole = whole + lax.ppermute(mine, ("store", "tensor"), pairs)
        column = whole.astype(BF16)
        shrunk = column
        for ds in range(2, n, 2):
            shrunk = shrunk + lax.ppermute(column, "store", [(s, (s + ds) % n) for s in range(n)])
        other = lax.ppermute(send, "tensor", swap)
        return final(shrunk, row_slot[:, None], factors, kept, other, owned)

    return shards


def solution(mesh):
    in_specs = (
        P(("parts", "store"), "tensor"),
        P("tensor", "store"),
        P(("parts", "store"), "tensor", None),
        P(("parts", "store"), None, None),
        P("parts"),
        P("parts"),
    )
    out_specs = P("parts", ("store", "tensor"))
    shards = make_shards(mesh.shape["store"], mesh.shape["tensor"])
    return jax.shard_map(shards, mesh=mesh, in_specs=in_specs, out_specs=out_specs, check_vma=False)
```
